32 devices in a mesh: dp: 8 (over z, y), tensor: 4 (over x, core).
Axes of the slice: x: 2, y: 2, z: 4, core: 2. Of those that a mesh axis runs over, the one named last changes fastest.
Arguments:
- momentum: bfloat16 [8, 512, 8192], P(None, 'dp', 'tensor'), may hold values from -125 to 125
- master: float32 [8, 512, 8192], P(None, 'dp', 'tensor'), may hold values from -0.06 to 0.06
- owner_order: int32 [8], replicated, may hold values from 0 to 7, each once
Outputs:
- new_master: float32 [8, 512, 8192], P(None, 'dp', 'tensor')
- owned_update: bfloat16 [8, 512, 8192], P('dp', None, 'tensor')
The draws below stay inside these ranges and needn't reach their ends.
Inputs may be any that keep to these rules, and one draw needn't show every extreme that they name: `owner_order`: each matrix appears in exactly one slot; slot j is owned by dp index j.
All inputs are finite; a program needn't handle non-finite values.
Results may differ from the reference program's by a relative error of at most 0.025.
Values may be sent and summed in bfloat16 or wider, within the bound.
A program may use at most 64 MiB of HBM per device.

```python
import math
import jax
import jax.numpy as jnp
from jax import lax

D = 8192
KV_DIM = 512
ITERS = 3
MATS = 8
COLS_DEV = 2048


def draw_momentum(key, part):
    subkeys = jax.random.split(jax.random.fold_in(key, 7), 3)
    full_shape = (MATS, KV_DIM, D)
    position = jnp.arange(D, dtype=jnp.float32) / D
    entries = jnp.clip(jax.random.normal(subkeys[0], full_shape, jnp.float32), -5.0, 5.0)
    row_scale = 10.0 ** jax.random.uniform(subkeys[1], (MATS, KV_DIM, 1), jnp.float32)
    column_ramp = 3.0 ** position
    column_scale = 10.0 ** jax.random.uniform(subkeys[2], (MATS, 1, D), jnp.float32) * column_ramp[None, None, :]
    return (entries * row_scale * column_scale / 20.0).astype(jnp.bfloat16)


def shard_levels(key, extent, cuts, low, high):
    factor_of, own = 1.0, jax.random.fold_in(key, 6)
    for dim, blocks in cuts:
        heights = jnp.exp(jax.random.uniform(jax.random.fold_in(own, dim), (blocks,), jnp.float32, low / len(cuts), high / len(cuts)))
        factor_of = factor_of * jnp.repeat(heights, extent[dim] // blocks).reshape([-1 if axis == dim else 1 for axis in range(len(extent))])
    return factor_of


def centred(rng, shape, scale, reach, cuts=(), kind=jnp.bfloat16):
    drawn = scale * jax.random.normal(rng, shape, jnp.float32)
    if cuts:
        drawn = drawn * shard_levels(rng, shape, cuts, -0.22, 0.18)
    return jnp.clip(drawn, -reach, reach).astype(kind)


def setup_inputs(seed: int = 0) -> dict:
    keys = jax.random.split(jax.random.key(seed), 4)
    return {
        "momentum": draw_momentum(jax.random.fold_in(keys[3], 71), 0),
        "master": centred(keys[1], (MATS, KV_DIM, D), 0.01, 0.06, ((1, 8), (2, 4)), jnp.float32),
        "owner_order": jax.random.permutation(keys[2], MATS).astype(jnp.int32),
    }


momentum_beta_unused = 0.95
learn_rate = 0.02
weight_decay = 0.1
norm_epsilon = 1e-07
quintic_first = 3.4445
quintic_second = -4.775
quintic_third = 2.0315

def block_gram(source):
    pieces = source.reshape(KV_DIM, D // COLS_DEV, COLS_DEV).astype(jnp.float32)
    partial_value = jnp.einsum('itk,jtk->tij', pieces, pieces)
    rounded = lax.optimization_barrier(partial_value.astype(jnp.bfloat16))
    return lax.optimization_barrier(jnp.sum(rounded.astype(jnp.float32), axis=0))

def orthogonalize(matrix):
    squares = jnp.sum(jnp.square(matrix.astype(jnp.float32)))
    inv_norm = 1.0 / (jnp.sqrt(squares) + norm_epsilon)
    current = (matrix.astype(jnp.float32) * inv_norm).astype(jnp.bfloat16)
    source = matrix
    combined = current.astype(jnp.float32)
    for iteration in range(ITERS):
        gram = block_gram(source)
        if iteration == 0:
            gram = gram * (inv_norm * inv_norm)
        coupling = gram.astype(jnp.bfloat16)
        first = jnp.dot(coupling, current, preferred_element_type=jnp.float32).astype(jnp.bfloat16)
        second = jnp.dot(coupling, first, preferred_element_type=jnp.float32)
        combined = quintic_first * current.astype(jnp.float32) + quintic_second * first.astype(jnp.float32) + quintic_third * second
        if iteration + 1 < ITERS:
            current = combined.astype(jnp.bfloat16)
            source = current
    scale_out = 0.2 * math.sqrt(max(KV_DIM, D))
    return (scale_out * combined).astype(jnp.bfloat16)

def reference(momentum, master, owner_order):

    def one_slot(index):
        return orthogonalize(lax.dynamic_index_in_dim(momentum, index, 0, keepdims=False))
    owned_update = lax.map(one_slot, owner_order)
    inverse = jnp.zeros((MATS,), jnp.int32).at[owner_order].set(jnp.arange(MATS, dtype=jnp.int32))
    by_matrix = jnp.take(owned_update, inverse, axis=0)
    new_master = master * (1.0 - learn_rate * weight_decay) - learn_rate * by_matrix.astype(jnp.float32)
    return (new_master, owned_update)
```

```python
import math

import jax
import jax.numpy as jnp
from jax import lax
from jax.sharding import PartitionSpec as P

learn_rate = 0.02
weight_decay = 0.1
norm_epsilon = 1e-07
quintic_first = 3.4445
quintic_second = -4.775
quintic_third = 2.0315
ITERS = 3


def halves(value):
    high = value.astype(jnp.bfloat16)
    low = (value - high.astype(jnp.float32)).astype(jnp.bfloat16)
    return high, low


def narrow_dot(left, right):
    return jnp.dot(left, right, preferred_element_type=jnp.float32)


def split_dot(left, right):
    return (
        narrow_dot(left[0], right[0]) + narrow_dot(left[0], right[1]) + narrow_dot(left[1], right[0])
    )


def polynomial(gram):
    size = gram.shape[0]
    eye = jnp.eye(size, dtype=jnp.float32)
    whole = None
    for step in range(ITERS):
        gram_halves = halves(gram)
        square = split_dot(gram_halves, gram_halves)
        factor = quintic_first * eye + quintic_second * gram + quintic_third * square
        factor_halves = halves(factor)
        whole = factor if whole is None else split_dot(factor_halves, halves(whole))
        if step + 1 < ITERS:
            gram = split_dot(halves(split_dot(factor_halves, gram_halves)), factor_halves)
    return whole


def plain_shards(scale_out, momentum, master, owner_order):
    matrices = momentum.shape[0]
    slotted = jnp.take(momentum, owner_order, axis=0)
    owned = lax.all_to_all(slotted, "dp", split_axis=0, concat_axis=1, tiled=True)

    def one(matrix):
        squares = lax.psum(jnp.sum(jnp.square(matrix.astype(jnp.float32))), "tensor")
        inv_norm = 1.0 / (jnp.sqrt(squares) + norm_epsilon)
        partial_value = lax.dot_general(
            matrix, matrix, (((1,), (1,)), ((), ())), preferred_element_type=jnp.float32
        )
        gram = lax.psum(partial_value.astype(jnp.bfloat16), "tensor").astype(jnp.float32)
        whole = polynomial(gram * (inv_norm * inv_norm)) * (scale_out * inv_norm)
        high, low = halves(whole)
        return (narrow_dot(high, matrix) + narrow_dot(low, matrix)).astype(jnp.bfloat16)

    owned_update = jnp.stack([one(owned[index]) for index in range(owned.shape[0])])
    returned = lax.all_to_all(owned_update, "dp", split_axis=1, concat_axis=0, tiled=True)
    inverse = (
        jnp.zeros((matrices,), jnp.int32).at[owner_order].set(jnp.arange(matrices, dtype=jnp.int32))
    )
    by_matrix = jnp.take(returned, inverse, axis=0)
    new_master = master * (1.0 - learn_rate * weight_decay) - learn_rate * by_matrix.astype(
        jnp.float32
    )
    return (new_master, owned_update)


def solution(mesh):
    def whole_call(momentum, master, owner_order):
        scale_out = 0.2 * math.sqrt(max(momentum.shape[1], momentum.shape[2]))

        def shards(momentum, master, owner_order):
            return plain_shards(scale_out, momentum, master, owner_order)

        return jax.shard_map(
            shards,
            mesh=mesh,
            in_specs=(P(None, "dp", "tensor"), P(None, "dp", "tensor"), P()),
            out_specs=(P(None, "dp", "tensor"), P("dp", None, "tensor")),
            check_vma=False,
        )(momentum, master, owner_order)

    return whole_call
```

```python
import functools
import math

import jax
import jax.numpy as jnp
from jax import lax
from jax.experimental import pallas as pl
from jax.experimental.pallas import tpu as pltpu
from jax.sharding import PartitionSpec as P

learn_rate = 0.02
weight_decay = 0.1
norm_epsilon = 1e-07
quintic_first = 3.4445
quintic_second = -4.775
quintic_third = 2.0315
ITERS = 3
MESH = pl.DeviceIdType.MESH


def halves(value):
    high = value.astype(jnp.bfloat16)
    low = (value - high.astype(jnp.float32)).astype(jnp.bfloat16)
    return high, low


def narrow_dot(left, right):
    return jnp.dot(left, right, preferred_element_type=jnp.float32)


def transposed_dot(left, right):
    return lax.dot_general(
        left, right, (((1,), (1,)), ((), ())), preferred_element_type=jnp.float32
    )


def far_first(count):
    return sorted(range(1, count), key=lambda offset: (abs(2 * offset - count), -offset))


def owner_kernel(
    n, rows, cols, chunk, scale_out,
    order_ref, mom_ref, ret_ref, upd_ref,
    send, recv, upd, gram, acc, part, part_in, half_out, half_in,
    gram_hi, gram_lo, fac_hi, fac_lo, all_hi, all_lo, tmp_hi, tmp_lo,
    in_send, in_recv, sum_send, sum_recv, out_send, out_recv, local_sem,
):
    me = lax.axis_index("dp")
    lane = lax.axis_index("tensor")
    core = lax.rem(lane, 2)
    mate = lane + 1 - 2 * core
    across = lax.rem(lane + 2, 4)
    size = n * rows
    half = size // 2
    chunks = cols // chunk

    barrier = pltpu.get_barrier_semaphore()
    for offset in range(1, n):
        pl.semaphore_signal(
            barrier, inc=1, device_id=(lax.rem(me + offset, n), lane), device_id_type=MESH
        )
    for other in (mate, across):
        pl.semaphore_signal(barrier, inc=1, device_id=(me, other), device_id_type=MESH)
    pl.semaphore_wait(barrier, n + 1)

    def rows_in(offset, index):
        place = pl.ds(index * chunk, chunk)
        return pltpu.make_async_remote_copy(
            src_ref=send.at[offset - 1, :, place],
            dst_ref=recv.at[me, :, place],
            send_sem=in_send.at[offset - 1, index],
            recv_sem=in_recv.at[offset - 1, index],
            device_id=(lax.rem(me + offset, n), lane),
            device_id_type=MESH,
        )

    for index in range(chunks):
        for offset in far_first(n):
            if index == 0:
                send[offset - 1] = mom_ref[order_ref[lax.rem(me + offset, n)]]
            rows_in(offset, index).start()
    recv[me] = mom_ref[order_ref[me]]

    acc[...] = jnp.zeros_like(acc)

    def add_chunk(index, carry):
        place = pl.ds(pl.multiple_of(index * chunk, chunk), chunk)
        for offset in range(1, n):
            pltpu.make_async_remote_copy(
                src_ref=send.at[offset - 1, :, place],
                dst_ref=recv.at[lax.rem(me + n - offset, n), :, place],
                send_sem=in_send.at[offset - 1, index],
                recv_sem=in_recv.at[offset - 1, index],
                device_id=(lax.rem(me + offset, n), lane),
                device_id_type=MESH,
            ).wait_recv()
        block = recv[:, :, place].reshape(size, chunk)
        for start in (0, half):
            acc[start : start + half, :] += transposed_dot(block[start : start + half], block)
        return carry

    lax.fori_loop(0, chunks, add_chunk, 0)

    part[...] = acc[...].astype(jnp.bfloat16)
    swap = pltpu.make_async_remote_copy(
        src_ref=part, dst_ref=part_in, send_sem=sum_send.at[0], recv_sem=sum_recv.at[0],
        device_id=(me, mate), device_id_type=MESH,
    )
    swap.start()
    swap.wait()
    mine = pl.ds(pl.multiple_of(core * half, half), half)
    half_out[...] = (
        part[mine, :].astype(jnp.float32) + part_in[mine, :].astype(jnp.float32)
    ).astype(jnp.bfloat16)
    swap = pltpu.make_async_remote_copy(
        src_ref=half_out, dst_ref=half_in, send_sem=sum_send.at[1], recv_sem=sum_recv.at[1],
        device_id=(me, across), device_id_type=MESH,
    )
    swap.start()
    swap.wait()
    gram[mine, :] = half_out[...].astype(jnp.float32) + half_in[...].astype(jnp.float32)
    swap = pltpu.make_async_remote_copy(
        src_ref=gram.at[mine, :], dst_ref=gram.at[mine, :],
        send_sem=sum_send.at[2], recv_sem=sum_recv.at[2],
        device_id=(me, mate), device_id_type=MESH,
    )
    swap.start()
    swap.wait()

    def diagonal(start):
        row = start + lax.broadcasted_iota(jnp.int32, (half, size), 0)
        return row == lax.broadcasted_iota(jnp.int32, (half, size), 1)

    strips = [(start, slice(start, start + half)) for start in (0, half)]
    squares = sum(
        jnp.sum(jnp.where(diagonal(start), gram[strip, :], 0.0), keepdims=True)
        for start, strip in strips
    )
    inv_norm = 1.0 / (jnp.sqrt(squares) + norm_epsilon)
    for start, strip in strips:
        scaled = gram[strip, :] * (inv_norm * inv_norm)
        acc[strip, :] = scaled
        gram_hi[strip, :], gram_lo[strip, :] = halves(scaled)

    for step in range(ITERS):
        last = step + 1 == ITERS
        for start, strip in strips:
            square = (
                narrow_dot(gram_hi[strip, :], gram_hi[...])
                + narrow_dot(gram_hi[strip, :], gram_lo[...])
                + narrow_dot(gram_lo[strip, :], gram_hi[...])
            )
            factor = quintic_second * acc[strip, :] + quintic_third * square
            factor += jnp.where(diagonal(start), quintic_first, 0.0)
            fac_hi[strip, :], fac_lo[strip, :] = halves(factor)
            if step == 0:
                all_hi[strip, :], all_lo[strip, :] = halves(factor)
        if not last:
            for start, strip in strips:
                tmp_hi[strip, :] = narrow_dot(fac_hi[strip, :], gram_hi[...]).astype(jnp.bfloat16)
            for start, strip in strips:
                following = narrow_dot(tmp_hi[strip, :], fac_hi[...])
                acc[strip, :] = following
                gram_hi[strip, :], gram_lo[strip, :] = halves(following)
        if step > 0:
            for start, strip in strips:
                joined = (
                    narrow_dot(fac_hi[strip, :], all_hi[...])
                    + narrow_dot(fac_hi[strip, :], all_lo[...])
                    + narrow_dot(fac_lo[strip, :], all_hi[...])
                )
                if last:
                    joined = joined * (scale_out * inv_norm)
                tmp_hi[strip, :], tmp_lo[strip, :] = halves(joined)
            if not last:
                all_hi[...] = tmp_hi[...]
                all_lo[...] = tmp_lo[...]

    def rows_out(dest):
        return pltpu.make_async_remote_copy(
            src_ref=upd.at[pl.ds(pl.multiple_of(dest * rows, rows), rows), :],
            dst_ref=ret_ref.at[me],
            send_sem=out_send.at[dest],
            recv_sem=out_recv.at[me],
            device_id=(dest, lane),
            device_id_type=MESH,
        )

    pairs = n // 2
    pair = lax.div(me, 2)
    twin = me + 1 - 2 * lax.rem(me, 2)
    for offset in far_first(pairs) + [0]:
        first = 2 * lax.rem(pair + offset, pairs)
        place = pl.ds(pl.multiple_of(first * rows, 2 * rows), 2 * rows)

        def apply_chunk(index, carry):
            lanes = pl.ds(pl.multiple_of(index * chunk, chunk), chunk)
            block = recv[:, :, lanes].reshape(size, chunk)
            upd[place, lanes] = (
                narrow_dot(tmp_hi[place, :], block) + narrow_dot(tmp_lo[place, :], block)
            ).astype(jnp.bfloat16)
            return carry

        lax.fori_loop(0, chunks, apply_chunk, 0)
        if offset:
            rows_out(first).start()
            rows_out(first + 1).start()
        else:
            rows_out(twin).start()
    own = pltpu.make_async_copy(
        upd.at[pl.ds(pl.multiple_of(me * rows, rows), rows), :], ret_ref.at[me], local_sem.at[0]
    )
    own.start()
    whole = pltpu.make_async_copy(upd, upd_ref, local_sem.at[1])
    whole.start()

    for index in range(chunks):
        for offset in range(1, n):
            rows_in(offset, index).wait_send()
    own.wait()
    whole.wait()
    for offset in range(1, n):
        dest = lax.rem(me + offset, n)
        rows_out(dest).wait_send()
        pltpu.make_async_remote_copy(
            src_ref=upd.at[pl.ds(pl.multiple_of(dest * rows, rows), rows), :],
            dst_ref=ret_ref.at[dest],
            send_sem=out_send.at[dest],
            recv_sem=out_recv.at[dest],
            device_id=(dest, lane),
            device_id_type=MESH,
        ).wait_recv()


def owner_call(scale_out, n, momentum, owner_order):
    rows, cols = momentum.shape[1:]
    size, half = n * rows, n * rows // 2
    chunk = cols // 4
    square_16 = pltpu.VMEM((size, size), jnp.bfloat16)
    square_32 = pltpu.VMEM((size, size), jnp.float32)
    half_16 = pltpu.VMEM((half, size), jnp.bfloat16)
    dma = pltpu.SemaphoreType.DMA
    return pl.pallas_call(
        functools.partial(owner_kernel, n, rows, cols, chunk, scale_out),
        out_shape=(
            jax.ShapeDtypeStruct((n, rows, cols), jnp.bfloat16),
            jax.ShapeDtypeStruct((size, cols), jnp.bfloat16),
        ),
        in_specs=[
            pl.BlockSpec(memory_space=pltpu.SMEM),
            pl.BlockSpec(memory_space=pltpu.VMEM),
        ],
        out_specs=(pl.BlockSpec(memory_space=pl.ANY), pl.BlockSpec(memory_space=pl.ANY)),
        scratch_shapes=[
            pltpu.VMEM((n - 1, rows, cols), jnp.bfloat16),
            pltpu.VMEM((n, rows, cols), jnp.bfloat16),
            pltpu.VMEM((size, cols), jnp.bfloat16),
            square_32, square_32, square_16, square_16, half_16, half_16,
            square_16, square_16, square_16, square_16, square_16, square_16, square_16, square_16,
            dma((n - 1, 4)), dma((n - 1, 4)), dma((3,)), dma((3,)), dma((n,)), dma((n,)), dma((2,)),
        ],
        compiler_params=pltpu.CompilerParams(
            collective_id=0, has_side_effects=True, vmem_limit_bytes=48 << 20
        ),
    )(owner_order, momentum)


def master_kernel(order_ref, ret_ref, master_ref, out_ref):
    out_ref[...] = master_ref[...] * (1.0 - learn_rate * weight_decay) - learn_rate * ret_ref[
        ...
    ].astype(jnp.float32)


def master_call(returned, master, owner_order):
    n, rows, cols = master.shape
    by_slot = pl.BlockSpec((1, rows, cols), lambda slot, order: (slot, 0, 0))
    by_matrix = pl.BlockSpec((1, rows, cols), lambda slot, order: (order[slot], 0, 0))
    return pl.pallas_call(
        master_kernel,
        out_shape=jax.ShapeDtypeStruct(master.shape, jnp.float32),
        grid_spec=pltpu.PrefetchScalarGridSpec(
            num_scalar_prefetch=1,
            grid=(n,),
            in_specs=[by_slot, by_matrix],
            out_specs=by_matrix,
        ),
        compiler_params=pltpu.CompilerParams(vmem_limit_bytes=32 << 20),
    )(owner_order, returned, master)


def kernel_shards(scale_out, n, momentum, master, owner_order):
    returned, owned_update = owner_call(scale_out, n, momentum, owner_order)
    return master_call(returned, master, owner_order), owned_update[None]


def wide_dot(left, right):
    return jnp.dot(left, right, precision=lax.Precision.HIGH)


def polynomial(gram):
    eye = jnp.eye(gram.shape[0], dtype=jnp.float32)
    whole = None
    for step in range(ITERS):
        factor = (
            quintic_first * eye + quintic_second * gram + quintic_third * wide_dot(gram, gram)
        )
        whole = factor if whole is None else wide_dot(factor, whole)
        if step + 1 < ITERS:
            gram = wide_dot(wide_dot(factor, gram), factor)
    return whole


def plain_shards(scale_out, momentum, master, owner_order):
    matrices = momentum.shape[0]
    slotted = jnp.take(momentum, owner_order, axis=0)
    owned = lax.all_to_all(slotted, "dp", split_axis=0, concat_axis=1, tiled=True)

    def one(matrix):
        squares = lax.psum(jnp.sum(jnp.square(matrix.astype(jnp.float32))), "tensor")
        inv_norm = 1.0 / (jnp.sqrt(squares) + norm_epsilon)
        partial_value = lax.dot_general(
            matrix, matrix, (((1,), (1,)), ((), ())), preferred_element_type=jnp.float32
        )
        gram = lax.psum(partial_value.astype(jnp.bfloat16), "tensor").astype(jnp.float32)
        whole = polynomial(gram * (inv_norm * inv_norm)) * (scale_out * inv_norm)
        return wide_dot(whole, matrix.astype(jnp.float32)).astype(jnp.bfloat16)

    owned_update = jnp.stack([one(owned[index]) for index in range(owned.shape[0])])
    returned = lax.all_to_all(owned_update, "dp", split_axis=1, concat_axis=0, tiled=True)
    inverse = (
        jnp.zeros((matrices,), jnp.int32).at[owner_order].set(jnp.arange(matrices, dtype=jnp.int32))
    )
    by_matrix = jnp.take(returned, inverse, axis=0)
    new_master = master * (1.0 - learn_rate * weight_decay) - learn_rate * by_matrix.astype(
        jnp.float32
    )
    return (new_master, owned_update)


def solution(mesh):
    n, lanes = mesh.shape["dp"], mesh.shape["tensor"]

    def whole_call(momentum, master, owner_order):
        scale_out = 0.2 * math.sqrt(max(momentum.shape[1], momentum.shape[2]))

        def shards(momentum, master, owner_order):
            matrices, rows, cols = momentum.shape
            if matrices == n and lanes == 4 and rows % 16 == 0 and cols % 512 == 0:
                return kernel_shards(scale_out, n, momentum, master, owner_order)
            return plain_shards(scale_out, momentum, master, owner_order)

        return jax.shard_map(
            shards,
            mesh=mesh,
            in_specs=(P(None, "dp", "tensor"), P(None, "dp", "tensor"), P()),
            out_specs=(P(None, "dp", "tensor"), P("dp", None, "tensor")),
            check_vma=False,
        )(momentum, master, owner_order)

    return whole_call
```

```python
import functools
import math

import jax
import jax.numpy as jnp
from jax import lax
from jax.experimental import pallas as pl
from jax.experimental.pallas import tpu as pltpu
from jax.sharding import PartitionSpec as P

learn_rate = 0.02
weight_decay = 0.1
norm_epsilon = 1e-07
quintic_first = 3.4445
quintic_second = -4.775
quintic_third = 2.0315
ITERS = 3
MESH = pl.DeviceIdType.MESH


def halves(value):
    high = value.astype(jnp.bfloat16)
    low = (value - high.astype(jnp.float32)).astype(jnp.bfloat16)
    return high, low


def narrow_dot(left, right):
    return jnp.dot(left, right, preferred_element_type=jnp.float32)


def transposed_dot(left, right):
    return lax.dot_general(
        left, right, (((1,), (1,)), ((), ())), preferred_element_type=jnp.float32
    )


def owner_kernel(
    n, rows, cols, chunk, scale_out,
    order_ref, mom_ref, ret_ref, upd_ref,
    send, recv, upd, gram, acc, part, part_in, half_out, half_in,
    gram_hi, gram_lo, fac_hi, fac_lo, all_hi, all_lo, tmp_hi, tmp_lo,
    in_send, in_recv, sum_send, sum_recv, out_send, out_recv, local_sem,
):
    me = lax.axis_index("dp")
    lane = lax.axis_index("tensor")
    core = lax.rem(lane, 2)
    mate = lane + 1 - 2 * core
    across = lax.rem(lane + 2, 4)
    size = n * rows
    half = size // 2
    chunks = cols // chunk

    barrier = pltpu.get_barrier_semaphore()
    for offset in range(1, n):
        pl.semaphore_signal(
            barrier, inc=1, device_id=(lax.rem(me + offset, n), lane), device_id_type=MESH
        )
    for other in (mate, across):
        pl.semaphore_signal(barrier, inc=1, device_id=(me, other), device_id_type=MESH)
    pl.semaphore_wait(barrier, n + 1)

    quarter = n // 4
    side = lax.div(me, 2 * quarter)

    def owner(stage, index):
        far = lax.rem(1 - side + index // quarter, 2)
        base = quarter + quarter * far if stage == 0 else 3 * quarter * far
        return base + lax.rem(me + index, quarter)

    def for_owners(stage, body):
        for index in range(2 * quarter):
            dest = owner(stage, index)

            @pl.when(dest != me)
            def _():
                body(stage * 2 * quarter + index, dest)

    def rows_in(slot, dest, index):
        place = pl.ds(index * chunk, chunk)
        return pltpu.make_async_remote_copy(
            src_ref=send.at[slot, :, place],
            dst_ref=recv.at[me, :, place],
            send_sem=in_send.at[slot, index],
            recv_sem=in_recv.at[me, index],
            device_id=(dest, lane),
            device_id_type=MESH,
        )

    def fill(slot, dest):
        send[slot] = mom_ref[order_ref[dest]]

    def start_chunk(index):
        return lambda slot, dest: rows_in(slot, dest, index).start()

    def finish_chunk(index):
        return lambda slot, dest: rows_in(slot, dest, index).wait_send()

    def fill_and_start(slot, dest):
        fill(slot, dest)
        rows_in(slot, dest, 0).start()

    for_owners(0, fill_and_start)
    for index in range(1, chunks):
        for_owners(0, start_chunk(index))
    for_owners(1, fill)
    recv[me] = mom_ref[order_ref[me]]
    for index in range(chunks - 1):
        for_owners(0, finish_chunk(index))
    for_owners(1, start_chunk(0))
    for_owners(0, finish_chunk(chunks - 1))
    for index in range(1, chunks):
        for_owners(1, start_chunk(index))

    acc[...] = jnp.zeros_like(acc)

    def add_chunk(index, carry):
        place = pl.ds(pl.multiple_of(index * chunk, chunk), chunk)
        for offset in range(1, n):
            source = lax.rem(me + offset, n)
            pltpu.make_async_remote_copy(
                src_ref=send.at[0, :, place],
                dst_ref=recv.at[source, :, place],
                send_sem=in_send.at[0, index],
                recv_sem=in_recv.at[source, index],
                device_id=(source, lane),
                device_id_type=MESH,
            ).wait_recv()
        block = recv[:, :, place].reshape(size, chunk)
        for start in (0, half):
            acc[start : start + half, :] += transposed_dot(block[start : start + half], block)
        return carry

    lax.fori_loop(0, chunks, add_chunk, 0)

    part[...] = acc[...].astype(jnp.bfloat16)
    swap = pltpu.make_async_remote_copy(
        src_ref=part, dst_ref=part_in, send_sem=sum_send.at[0], recv_sem=sum_recv.at[0],
        device_id=(me, mate), device_id_type=MESH,
    )
    swap.start()
    swap.wait()
    mine = pl.ds(pl.multiple_of(core * half, half), half)
    half_out[...] = (
        part[mine, :].astype(jnp.float32) + part_in[mine, :].astype(jnp.float32)
    ).astype(jnp.bfloat16)
    swap = pltpu.make_async_remote_copy(
        src_ref=half_out, dst_ref=half_in, send_sem=sum_send.at[1], recv_sem=sum_recv.at[1],
        device_id=(me, across), device_id_type=MESH,
    )
    swap.start()
    swap.wait()
    gram[mine, :] = half_out[...].astype(jnp.float32) + half_in[...].astype(jnp.float32)
    swap = pltpu.make_async_remote_copy(
        src_ref=gram.at[mine, :], dst_ref=gram.at[mine, :],
        send_sem=sum_send.at[2], recv_sem=sum_recv.at[2],
        device_id=(me, mate), device_id_type=MESH,
    )
    swap.start()
    swap.wait()

    def diagonal(start):
        row = start + lax.broadcasted_iota(jnp.int32, (half, size), 0)
        return row == lax.broadcasted_iota(jnp.int32, (half, size), 1)

    strips = [(start, slice(start, start + half)) for start in (0, half)]
    squares = sum(
        jnp.sum(jnp.where(diagonal(start), gram[strip, :], 0.0), keepdims=True)
        for start, strip in strips
    )
    inv_norm = 1.0 / (jnp.sqrt(squares) + norm_epsilon)
    for start, strip in strips:
        scaled = gram[strip, :] * (inv_norm * inv_norm)
        acc[strip, :] = scaled
        gram_hi[strip, :], gram_lo[strip, :] = halves(scaled)

    def joined(strip):
        return (
            narrow_dot(fac_hi[strip, :], all_hi[...])
            + narrow_dot(fac_hi[strip, :], all_lo[...])
            + narrow_dot(fac_lo[strip, :], all_hi[...])
        )

    for step in range(ITERS):
        last = step + 1 == ITERS
        for start, strip in strips:
            square = (
                narrow_dot(gram_hi[strip, :], gram_hi[...])
                + narrow_dot(gram_hi[strip, :], gram_lo[...])
                + narrow_dot(gram_lo[strip, :], gram_hi[...])
            )
            factor = quintic_second * acc[strip, :] + quintic_third * square
            factor += jnp.where(diagonal(start), quintic_first, 0.0)
            fac_hi[strip, :], fac_lo[strip, :] = halves(factor)
            if step == 0:
                all_hi[strip, :], all_lo[strip, :] = halves(factor)
        if not last:
            for start, strip in strips:
                tmp_hi[strip, :] = narrow_dot(fac_hi[strip, :], gram_hi[...]).astype(jnp.bfloat16)
            for start, strip in strips:
                following = narrow_dot(tmp_hi[strip, :], fac_hi[...])
                acc[strip, :] = following
                gram_hi[strip, :], gram_lo[strip, :] = halves(following)
        if step > 0 and not last:
            for start, strip in strips:
                tmp_hi[strip, :], tmp_lo[strip, :] = halves(joined(strip))
            all_hi[...] = tmp_hi[...]
            all_lo[...] = tmp_lo[...]

    def rows_out(dest):
        return pltpu.make_async_remote_copy(
            src_ref=upd.at[pl.ds(pl.multiple_of(dest * rows, rows), rows), :],
            dst_ref=ret_ref.at[me],
            send_sem=out_send.at[dest],
            recv_sem=out_recv.at[me],
            device_id=(dest, lane),
            device_id_type=MESH,
        )

    pairs_side = n // 4
    pair = lax.div(me, 2)
    twin = me + 1 - 2 * lax.rem(me, 2)
    for part in (0, 1):
        target = 1 - side if part == 0 else side
        strip = pl.ds(pl.multiple_of(target * half, half), half)
        tmp_hi[strip, :], tmp_lo[strip, :] = halves(joined(strip) * (scale_out * inv_norm))
        for index in range(pairs_side):
            step = (index + part) % pairs_side
            first = 2 * (target * pairs_side + lax.rem(pair + step, pairs_side))
            place = pl.ds(pl.multiple_of(first * rows, 2 * rows), 2 * rows)

            def apply_chunk(index, carry, place=place):
                lanes = pl.ds(pl.multiple_of(index * chunk, chunk), chunk)
                block = recv[:, :, lanes].reshape(size, chunk)
                upd[place, lanes] = (
                    narrow_dot(tmp_hi[place, :], block) + narrow_dot(tmp_lo[place, :], block)
                ).astype(jnp.bfloat16)
                return carry

            lax.fori_loop(0, chunks, apply_chunk, 0)
            if part == 1 and step == 0:
                rows_out(twin).start()
            else:
                rows_out(first).start()
                rows_out(first + 1).start()
    own = pltpu.make_async_copy(
        upd.at[pl.ds(pl.multiple_of(me * rows, rows), rows), :], ret_ref.at[me], local_sem.at[0]
    )
    own.start()
    whole = pltpu.make_async_copy(upd, upd_ref, local_sem.at[1])
    whole.start()

    for index in range(chunks):
        for_owners(1, finish_chunk(index))
    own.wait()
    whole.wait()
    for offset in range(1, n):
        dest = lax.rem(me + offset, n)
        rows_out(dest).wait_send()
        pltpu.make_async_remote_copy(
            src_ref=upd.at[pl.ds(pl.multiple_of(dest * rows, rows), rows), :],
            dst_ref=ret_ref.at[dest],
            send_sem=out_send.at[dest],
            recv_sem=out_recv.at[dest],
            device_id=(dest, lane),
            device_id_type=MESH,
        ).wait_recv()


def owner_call(scale_out, n, momentum, owner_order):
    rows, cols = momentum.shape[1:]
    size, half = n * rows, n * rows // 2
    chunk = cols // 4
    square_16 = pltpu.VMEM((size, size), jnp.bfloat16)
    square_32 = pltpu.VMEM((size, size), jnp.float32)
    half_16 = pltpu.VMEM((half, size), jnp.bfloat16)
    dma = pltpu.SemaphoreType.DMA
    return pl.pallas_call(
        functools.partial(owner_kernel, n, rows, cols, chunk, scale_out),
        out_shape=(
            jax.ShapeDtypeStruct((n, rows, cols), jnp.bfloat16),
            jax.ShapeDtypeStruct((size, cols), jnp.bfloat16),
        ),
        in_specs=[
            pl.BlockSpec(memory_space=pltpu.SMEM),
            pl.BlockSpec(memory_space=pltpu.VMEM),
        ],
        out_specs=(pl.BlockSpec(memory_space=pl.ANY), pl.BlockSpec(memory_space=pl.ANY)),
        scratch_shapes=[
            pltpu.VMEM((n, rows, cols), jnp.bfloat16),
            pltpu.VMEM((n, rows, cols), jnp.bfloat16),
            pltpu.VMEM((size, cols), jnp.bfloat16),
            square_32, square_32, square_16, square_16, half_16, half_16,
            square_16, square_16, square_16, square_16, square_16, square_16, square_16, square_16,
            dma((n, 4)), dma((n, 4)), dma((3,)), dma((3,)), dma((n,)), dma((n,)), dma((2,)),
        ],
        compiler_params=pltpu.CompilerParams(
            collective_id=0, has_side_effects=True, vmem_limit_bytes=30 << 20
        ),
        cost_estimate=pl.CostEstimate(
            flops=6 * size * size * cols + 40 * size**3,
            bytes_accessed=12 * size * cols,
            transcendentals=0,
        ),
    )(owner_order, momentum)


def master_kernel(n, order_ref, ret_ref, upd_ref, master_ref, out_ref, upd_out_ref, fresh, sems):
    whole = pltpu.make_async_copy(upd_ref, upd_out_ref, sems.at[n])
    copies = []
    for slot in range(n):
        matrix = order_ref[slot]
        fresh[slot] = master_ref[matrix] * (1.0 - learn_rate * weight_decay) - learn_rate * ret_ref[
            slot
        ].astype(jnp.float32)
        copies.append(pltpu.make_async_copy(fresh.at[slot], out_ref.at[matrix], sems.at[slot]))
        copies[-1].start()
        if slot == 0:
            whole.start()
    for copy in copies + [whole]:
        copy.wait()


def master_call(returned, update, master, owner_order):
    n = master.shape[0]
    vmem = pl.BlockSpec(memory_space=pltpu.VMEM)
    hbm = pl.BlockSpec(memory_space=pl.ANY)
    return pl.pallas_call(
        functools.partial(master_kernel, n),
        out_shape=(
            jax.ShapeDtypeStruct(master.shape, jnp.float32),
            jax.ShapeDtypeStruct(update.shape, update.dtype),
        ),
        in_specs=[pl.BlockSpec(memory_space=pltpu.SMEM), vmem, vmem, vmem],
        out_specs=(hbm, hbm),
        scratch_shapes=[
            pltpu.VMEM(master.shape, jnp.float32), pltpu.SemaphoreType.DMA((n + 1,))
        ],
        compiler_params=pltpu.CompilerParams(vmem_limit_bytes=24 << 20),
    )(owner_order, returned, update, master)


def kernel_shards(scale_out, n, momentum, master, owner_order):
    returned, owned_update = owner_call(scale_out, n, momentum, owner_order)
    new_master, owned_update = master_call(returned, owned_update, master, owner_order)
    return new_master, owned_update[None]


def wide_dot(left, right):
    return jnp.dot(left, right, precision=lax.Precision.HIGH)


def polynomial(gram):
    eye = jnp.eye(gram.shape[0], dtype=jnp.float32)
    whole = None
    for step in range(ITERS):
        factor = (
            quintic_first * eye + quintic_second * gram + quintic_third * wide_dot(gram, gram)
        )
        whole = factor if whole is None else wide_dot(factor, whole)
        if step + 1 < ITERS:
            gram = wide_dot(wide_dot(factor, gram), factor)
    return whole


def plain_shards(scale_out, momentum, master, owner_order):
    matrices = momentum.shape[0]
    slotted = jnp.take(momentum, owner_order, axis=0)
    owned = lax.all_to_all(slotted, "dp", split_axis=0, concat_axis=1, tiled=True)

    def one(matrix):
        squares = lax.psum(jnp.sum(jnp.square(matrix.astype(jnp.float32))), "tensor")
        inv_norm = 1.0 / (jnp.sqrt(squares) + norm_epsilon)
        partial_value = lax.dot_general(
            matrix, matrix, (((1,), (1,)), ((), ())), preferred_element_type=jnp.float32
        )
        gram = lax.psum(partial_value.astype(jnp.bfloat16), "tensor").astype(jnp.float32)
        whole = polynomial(gram * (inv_norm * inv_norm)) * (scale_out * inv_norm)
        return wide_dot(whole, matrix.astype(jnp.float32)).astype(jnp.bfloat16)

    owned_update = jnp.stack([one(owned[index]) for index in range(owned.shape[0])])
    returned = lax.all_to_all(owned_update, "dp", split_axis=1, concat_axis=0, tiled=True)
    inverse = (
        jnp.zeros((matrices,), jnp.int32).at[owner_order].set(jnp.arange(matrices, dtype=jnp.int32))
    )
    by_matrix = jnp.take(returned, inverse, axis=0)
    new_master = master * (1.0 - learn_rate * weight_decay) - learn_rate * by_matrix.astype(
        jnp.float32
    )
    return (new_master, owned_update)


def solution(mesh):
    n, lanes = mesh.shape["dp"], mesh.shape["tensor"]

    def whole_call(momentum, master, owner_order):
        scale_out = 0.2 * math.sqrt(max(momentum.shape[1], momentum.shape[2]))

        def shards(momentum, master, owner_order):
            matrices, rows, cols = momentum.shape
            if matrices == n and lanes == 4 and n % 4 == 0 and rows % 16 == 0 and cols % 512 == 0:
                return kernel_shards(scale_out, n, momentum, master, owner_order)
            return plain_shards(scale_out, momentum, master, owner_order)

        return jax.shard_map(
            shards,
            mesh=mesh,
            in_specs=(P(None, "dp", "tensor"), P(None, "dp", "tensor"), P()),
            out_specs=(P(None, "dp", "tensor"), P("dp", None, "tensor")),
            check_vma=False,
        )(momentum, master, owner_order)

    return whole_call
```

```python
import functools
import math

import jax
import jax.numpy as jnp
from jax import lax
from jax.experimental import pallas as pl
from jax.experimental.pallas import tpu as pltpu
from jax.sharding import PartitionSpec as P

learn_rate = 0.02
weight_decay = 0.1
norm_epsilon = 1e-07
quintic_first = 3.4445
quintic_second = -4.775
quintic_third = 2.0315
ITERS = 3
MESH = pl.DeviceIdType.MESH


def halves(value):
    high = value.astype(jnp.bfloat16)
    low = (value - high.astype(jnp.float32)).astype(jnp.bfloat16)
    return high, low


def narrow_dot(left, right):
    return jnp.dot(left, right, preferred_element_type=jnp.float32)


def transposed_dot(left, right):
    return lax.dot_general(
        left, right, (((1,), (1,)), ((), ())), preferred_element_type=jnp.float32
    )


def visit_order(n):
    last = [n - 2, 2]
    near = [n - 1, 1]
    rest = [offset for offset in range(1, n) if offset not in last + near]
    return sorted(rest, key=lambda offset: (abs(offset - n // 2), offset)) + near + last


def owner_kernel(
    n, rows, cols, chunk, scale_out,
    order_ref, mom_ref, ret_ref, upd_ref,
    send, recv, upd, gram,
    early, early_part, early_in, early_half, early_half_in, early_sum,
    late, late_part, late_in, late_half, late_half_in, late_sum,
    gram_left, gram_right, fac_left, all_right, passing, mixed,
    in_send, in_recv, sum_send, sum_recv, out_send, out_recv, own_sem, write_sem,
):
    me = lax.axis_index("dp")
    lane = lax.axis_index("tensor")
    core = lax.rem(lane, 2)
    mate = lane + 1 - 2 * core
    across = lax.rem(lane + 2, 4)
    size = n * rows
    half = size // 2
    first = size - 2 * rows
    chunks = cols // chunk
    order = visit_order(n)

    barrier = pltpu.get_barrier_semaphore()
    for offset in range(1, n):
        pl.semaphore_signal(
            barrier, inc=1, device_id=(lax.rem(me + offset, n), lane), device_id_type=MESH
        )
    for other in (mate, across):
        pl.semaphore_signal(barrier, inc=1, device_id=(me, other), device_id_type=MESH)
    pl.semaphore_wait(barrier, n + 1)

    def rows_in(slot):
        return pltpu.make_async_remote_copy(
            src_ref=send.at[slot],
            dst_ref=recv.at[slot],
            send_sem=in_send.at[slot],
            recv_sem=in_recv.at[slot],
            device_id=(lax.rem(me + order[slot - 1], n), lane),
            device_id_type=MESH,
        )

    def holder(slot):
        return lax.rem(me + n - order[slot - 1], n) if slot else me

    for slot in range(1, n):
        send[slot] = mom_ref[order_ref[lax.rem(me + order[slot - 1], n)]]
        rows_in(slot).start()
    recv[0] = mom_ref[order_ref[me]]

    def columns(index, start, count):
        place = pl.ds(pl.multiple_of(index * chunk, chunk), chunk)
        return recv[start : start + count, :, place].reshape(count * rows, chunk)

    def tensor_sum(total, part, part_in, half_out, half_in, summed, sem):
        count = total.shape[0] // 2
        mine = pl.ds(pl.multiple_of(core * count, count), count)

        def swap(step, source, target, other):
            copy = pltpu.make_async_remote_copy(
                src_ref=source, dst_ref=target,
                send_sem=sum_send.at[sem + step], recv_sem=sum_recv.at[sem + step],
                device_id=(me, other), device_id_type=MESH,
            )
            copy.start()
            copy.wait()

        part[...] = total[...].astype(jnp.bfloat16)
        swap(0, part, part_in, mate)
        half_out[...] = (
            part[mine, :].astype(jnp.float32) + part_in[mine, :].astype(jnp.float32)
        ).astype(jnp.bfloat16)
        swap(1, half_out, half_in, across)
        summed[mine, :] = half_out[...].astype(jnp.float32) + half_in[...].astype(jnp.float32)
        swap(2, summed.at[mine, :], summed.at[mine, :], mate)

    for slot in range(1, n - 2):
        rows_in(slot).wait_recv()
    early[...] = jnp.zeros_like(early)

    def add_early(index, carry):
        block = columns(index, 0, n - 2)
        for start in (0, first // 2):
            early[start : start + first // 2, :] += transposed_dot(
                block[start : start + first // 2], block
            )
        return carry

    lax.fori_loop(0, chunks, add_early, 0)
    tensor_sum(early, early_part, early_in, early_half, early_half_in, early_sum, 0)

    for slot in (n - 2, n - 1):
        rows_in(slot).wait_recv()
    late[...] = jnp.zeros_like(late)

    def add_late(index, carry):
        late[...] += transposed_dot(columns(index, n - 2, 2), columns(index, 0, n))
        return carry

    lax.fori_loop(0, chunks, add_late, 0)
    tensor_sum(late, late_part, late_in, late_half, late_half_in, late_sum, 3)

    def diagonal(height, width, start):
        row = start + lax.broadcasted_iota(jnp.int32, (height, width), 0)
        return row == lax.broadcasted_iota(jnp.int32, (height, width), 1)

    def trace(value, start):
        return jnp.sum(jnp.where(diagonal(*value.shape, start), value, 0.0), keepdims=True)

    squares = trace(early_sum[...], 0) + trace(late_sum[...], first)
    inv_norm = 1.0 / (jnp.sqrt(squares) + norm_epsilon)
    square_scale = inv_norm * inv_norm
    gram[:first, :first] = early_sum[...] * square_scale
    gram[first:, :] = late_sum[...] * square_scale
    gram[:first, first:] = late_sum[:, :first].T * square_scale

    strips = [(start, slice(start, start + half)) for start in (0, half)]

    def as_left(target, strip, value):
        high, low = halves(value)
        target[strip, 0:size] = high
        target[strip, size : 2 * size] = high
        target[strip, 2 * size :] = low

    def as_right(target, start, value):
        high, low = halves(value)
        target[start : start + half, :] = high
        target[size + start : size + start + half, :] = low
        target[2 * size + start : 2 * size + start + half, :] = high

    for start, strip in strips:
        as_left(gram_left, strip, gram[strip, :])
        as_right(gram_right, start, gram[strip, :])

    for step in range(ITERS):
        last = step + 1 == ITERS
        for start, strip in strips:
            factor = quintic_second * gram[strip, :] + quintic_third * narrow_dot(
                gram_left[strip, :], gram_right[...]
            )
            factor += jnp.where(diagonal(half, size, start), quintic_first, 0.0)
            as_left(fac_left, strip, factor)
            if step == 0:
                as_right(all_right, start, factor)
        if not last:
            for start, strip in strips:
                mixed[strip, :] = narrow_dot(
                    fac_left[strip, :size], gram_right[:size, :]
                ).astype(jnp.bfloat16)
            for start, strip in strips:
                following = narrow_dot(mixed[strip, :], fac_left[:, :size])
                gram[strip, :] = following
                as_left(gram_left, strip, following)
                as_right(gram_right, start, following)
        if 0 < step and not last:
            for start, strip in strips:
                passing[strip, :] = narrow_dot(fac_left[strip, :], all_right[...])
            for start, strip in strips:
                as_right(all_right, start, passing[strip, :])

    def rows_out(slot):
        return pltpu.make_async_remote_copy(
            src_ref=upd.at[slot * rows : (slot + 1) * rows, :],
            dst_ref=ret_ref.at[me],
            send_sem=out_send.at[slot],
            recv_sem=out_recv.at[me],
            device_id=(holder(slot), lane),
            device_id_type=MESH,
        )

    def write(slot):
        place = pl.ds(pl.multiple_of(holder(slot) * rows, rows), rows)
        return pltpu.make_async_copy(
            upd.at[slot * rows : (slot + 1) * rows, :], upd_ref.at[place, :], write_sem.at[slot]
        )

    own = pltpu.make_async_copy(upd.at[0:rows, :], ret_ref.at[me], own_sem.at[0])
    for start, strip in strips:
        high, low = halves(
            narrow_dot(fac_left[strip, :], all_right[...]) * (scale_out * inv_norm)
        )
        mixed[strip, :] = high
        fac_left[strip, :size] = low
        for top in range(start, start + half, 2 * rows):

            def apply_chunk(index, carry, top=top):
                place = pl.ds(pl.multiple_of(index * chunk, chunk), chunk)
                block = columns(index, 0, n)
                upd[top : top + 2 * rows, place] = (
                    narrow_dot(mixed[top : top + 2 * rows, :], block)
                    + narrow_dot(fac_left[top : top + 2 * rows, :size], block)
                ).astype(jnp.bfloat16)
                return carry

            lax.fori_loop(0, chunks, apply_chunk, 0)
            for slot in (top // rows, top // rows + 1):
                if slot:
                    rows_out(slot).start()
                else:
                    own.start()
    for slot in range(n):
        write(slot).start()

    for slot in range(1, n):
        rows_in(slot).wait_send()
    own.wait()
    for slot in range(n):
        write(slot).wait()
    for slot in range(1, n):
        rows_out(slot).wait_send()
        source = lax.rem(me + slot, n)
        pltpu.make_async_remote_copy(
            src_ref=upd.at[0:rows, :],
            dst_ref=ret_ref.at[source],
            send_sem=out_send.at[slot],
            recv_sem=out_recv.at[source],
            device_id=(source, lane),
            device_id_type=MESH,
        ).wait_recv()


def owner_call(scale_out, n, momentum, owner_order):
    rows, cols = momentum.shape[1:]
    size, first, strip = n * rows, (n - 2) * rows, 2 * rows

    def wide(*shape):
        return pltpu.VMEM(shape, jnp.float32)

    def narrow(*shape):
        return pltpu.VMEM(shape, jnp.bfloat16)

    def gram_buffers(height, width):
        return [
            wide(height, width), narrow(height, width), narrow(height, width),
            narrow(height // 2, width), narrow(height // 2, width), wide(height, width),
        ]

    dma = pltpu.SemaphoreType.DMA
    return pl.pallas_call(
        functools.partial(owner_kernel, n, rows, cols, cols // 4, scale_out),
        out_shape=(
            jax.ShapeDtypeStruct((n, rows, cols), jnp.bfloat16),
            jax.ShapeDtypeStruct((size, cols), jnp.bfloat16),
        ),
        in_specs=[
            pl.BlockSpec(memory_space=pltpu.SMEM),
            pl.BlockSpec(memory_space=pltpu.VMEM),
        ],
        out_specs=(pl.BlockSpec(memory_space=pl.ANY), pl.BlockSpec(memory_space=pl.ANY)),
        scratch_shapes=[
            narrow(n, rows, cols), narrow(n, rows, cols), narrow(size, cols), wide(size, size),
            *gram_buffers(first, first),
            *gram_buffers(strip, size),
            narrow(size, 3 * size), narrow(3 * size, size), narrow(size, 3 * size),
            narrow(3 * size, size), wide(size, size), narrow(size, size),
            dma((n,)), dma((n,)), dma((6,)), dma((6,)), dma((n,)), dma((n,)), dma((1,)), dma((n,)),
        ],
        compiler_params=pltpu.CompilerParams(
            collective_id=0, has_side_effects=True, vmem_limit_bytes=32 << 20
        ),
        cost_estimate=pl.CostEstimate(
            flops=6 * size * size * cols + 40 * size**3,
            bytes_accessed=12 * size * cols,
            transcendentals=0,
        ),
    )(owner_order, momentum)


def master_kernel(n, order_ref, ret_ref, upd_ref, master_ref, out_ref, upd_out_ref, fresh, sems):
    whole = pltpu.make_async_copy(upd_ref, upd_out_ref, sems.at[n])
    copies = []
    for slot in range(n):
        matrix = order_ref[slot]
        fresh[slot] = master_ref[matrix] * (1.0 - learn_rate * weight_decay) - learn_rate * ret_ref[
            slot
        ].astype(jnp.float32)
        copies.append(pltpu.make_async_copy(fresh.at[slot], out_ref.at[matrix], sems.at[slot]))
        copies[-1].start()
        if slot == 0:
            whole.start()
    for copy in copies + [whole]:
        copy.wait()


def master_call(returned, update, master, owner_order):
    n = master.shape[0]
    vmem = pl.BlockSpec(memory_space=pltpu.VMEM)
    hbm = pl.BlockSpec(memory_space=pl.ANY)
    return pl.pallas_call(
        functools.partial(master_kernel, n),
        out_shape=(
            jax.ShapeDtypeStruct(master.shape, jnp.float32),
            jax.ShapeDtypeStruct(update.shape, update.dtype),
        ),
        in_specs=[pl.BlockSpec(memory_space=pltpu.SMEM), vmem, vmem, vmem],
        out_specs=(hbm, hbm),
        scratch_shapes=[
            pltpu.VMEM(master.shape, jnp.float32), pltpu.SemaphoreType.DMA((n + 1,))
        ],
        compiler_params=pltpu.CompilerParams(vmem_limit_bytes=24 << 20),
    )(owner_order, returned, update, master)


def kernel_shards(scale_out, n, momentum, master, owner_order):
    returned, owned_update = owner_call(scale_out, n, momentum, owner_order)
    new_master, owned_update = master_call(returned, owned_update, master, owner_order)
    return new_master, owned_update[None]


def wide_dot(left, right):
    return jnp.dot(left, right, precision=lax.Precision.HIGH)


def polynomial(gram):
    eye = jnp.eye(gram.shape[0], dtype=jnp.float32)
    whole = None
    for step in range(ITERS):
        factor = (
            quintic_first * eye + quintic_second * gram + quintic_third * wide_dot(gram, gram)
        )
        whole = factor if whole is None else wide_dot(factor, whole)
        if step + 1 < ITERS:
            gram = wide_dot(wide_dot(factor, gram), factor)
    return whole


def plain_shards(scale_out, momentum, master, owner_order):
    matrices = momentum.shape[0]
    slotted = jnp.take(momentum, owner_order, axis=0)
    owned = lax.all_to_all(slotted, "dp", split_axis=0, concat_axis=1, tiled=True)

    def one(matrix):
        squares = lax.psum(jnp.sum(jnp.square(matrix.astype(jnp.float32))), "tensor")
        inv_norm = 1.0 / (jnp.sqrt(squares) + norm_epsilon)
        partial_value = lax.dot_general(
            matrix, matrix, (((1,), (1,)), ((), ())), preferred_element_type=jnp.float32
        )
        gram = lax.psum(partial_value.astype(jnp.bfloat16), "tensor").astype(jnp.float32)
        whole = polynomial(gram * (inv_norm * inv_norm)) * (scale_out * inv_norm)
        return wide_dot(whole, matrix.astype(jnp.float32)).astype(jnp.bfloat16)

    owned_update = jnp.stack([one(owned[index]) for index in range(owned.shape[0])])
    returned = lax.all_to_all(owned_update, "dp", split_axis=1, concat_axis=0, tiled=True)
    inverse = (
        jnp.zeros((matrices,), jnp.int32).at[owner_order].set(jnp.arange(matrices, dtype=jnp.int32))
    )
    by_matrix = jnp.take(returned, inverse, axis=0)
    new_master = master * (1.0 - learn_rate * weight_decay) - learn_rate * by_matrix.astype(
        jnp.float32
    )
    return (new_master, owned_update)


def solution(mesh):
    n, lanes = mesh.shape["dp"], mesh.shape["tensor"]

    def whole_call(momentum, master, owner_order):
        scale_out = 0.2 * math.sqrt(max(momentum.shape[1], momentum.shape[2]))

        def shards(momentum, master, owner_order):
            matrices, rows, cols = momentum.shape
            if matrices == n and lanes == 4 and n >= 8 and n % 4 == 0 and rows % 64 == 0 and cols % 512 == 0:
                return kernel_shards(scale_out, n, momentum, master, owner_order)
            return plain_shards(scale_out, momentum, master, owner_order)

        return jax.shard_map(
            shards,
            mesh=mesh,
            in_specs=(P(None, "dp", "tensor"), P(None, "dp", "tensor"), P()),
            out_specs=(P(None, "dp", "tensor"), P("dp", None, "tensor")),
            check_vma=False,
        )(momentum, master, owner_order)

    return whole_call
```

```python
import functools
import math

import jax
import jax.numpy as jnp
from jax import lax
from jax.experimental import pallas as pl
from jax.experimental.pallas import tpu as pltpu
from jax.sharding import PartitionSpec as P

learn_rate = 0.02
weight_decay = 0.1
norm_epsilon = 1e-07
quintic_first = 3.4445
quintic_second = -4.775
quintic_third = 2.0315
ITERS = 3
MESH = pl.DeviceIdType.MESH


def halves(value):
    high = value.astype(jnp.bfloat16)
    low = (value - high.astype(jnp.float32)).astype(jnp.bfloat16)
    return high, low


def narrow_dot(left, right):
    return jnp.dot(left, right, preferred_element_type=jnp.float32)


def transposed_dot(left, right):
    return lax.dot_general(
        left, right, (((1,), (1,)), ((), ())), preferred_element_type=jnp.float32
    )


def visit_order(n):
    last = [n - 2, 2]
    rest = [offset for offset in range(1, n) if offset not in last]
    rest.sort(key=lambda offset: (abs(offset - n // 2), offset))
    count = len(rest)
    mixed = [rest[index // 2 if index % 2 == 0 else count - 1 - index // 2] for index in range(count)]
    return mixed + last


def owner_kernel(
    n, rows, cols, chunk, scale_out,
    order_ref, mom_ref, ret_ref, upd_ref,
    send, recv, upd, gram,
    early, early_part, early_in, early_half, early_half_in, early_sum,
    late, late_part, late_in, late_half, late_half_in, late_sum,
    gram_left, gram_right, fac_left, all_right, passing, mixed,
    in_send, in_recv, sum_send, sum_recv, out_send, out_recv, own_sem, write_sem,
):
    me = lax.axis_index("dp")
    lane = lax.axis_index("tensor")
    core = lax.rem(lane, 2)
    mate = lane + 1 - 2 * core
    across = lax.rem(lane + 2, 4)
    size = n * rows
    half = size // 2
    first = size - 2 * rows
    chunks = cols // chunk
    order = visit_order(n)

    barrier = pltpu.get_barrier_semaphore()
    for offset in range(1, n):
        pl.semaphore_signal(
            barrier, inc=1, device_id=(lax.rem(me + offset, n), lane), device_id_type=MESH
        )
    for other in (mate, across):
        pl.semaphore_signal(barrier, inc=1, device_id=(me, other), device_id_type=MESH)
    pl.semaphore_wait(barrier, n + 1)

    def lanes_of(index):
        return pl.ds(pl.multiple_of(index * chunk, chunk), chunk)

    def rows_in(slot, index):
        return pltpu.make_async_remote_copy(
            src_ref=send.at[slot, :, lanes_of(index)],
            dst_ref=recv.at[slot, :, lanes_of(index)],
            send_sem=in_send.at[slot, index],
            recv_sem=in_recv.at[slot, index],
            device_id=(lax.rem(me + order[slot - 1], n), lane),
            device_id_type=MESH,
        )

    def holder(slot):
        return lax.rem(me + n - order[slot - 1], n) if slot else me

    for slots in (range(1, n - 2), range(n - 2, n)):
        for index in range(chunks):
            for slot in slots:
                if index == 0:
                    send[slot] = mom_ref[order_ref[lax.rem(me + order[slot - 1], n)]]
                rows_in(slot, index).start()
    recv[0] = mom_ref[order_ref[me]]

    def columns(index, start, count):
        return recv[start : start + count, :, lanes_of(index)].reshape(count * rows, chunk)

    def tensor_sum(total, part, part_in, half_out, half_in, summed, sem):
        count = total.shape[0] // 2
        mine = pl.ds(pl.multiple_of(core * count, count), count)

        def swap(step, source, target, other):
            copy = pltpu.make_async_remote_copy(
                src_ref=source, dst_ref=target,
                send_sem=sum_send.at[sem + step], recv_sem=sum_recv.at[sem + step],
                device_id=(me, other), device_id_type=MESH,
            )
            copy.start()
            copy.wait()

        part[...] = total[...].astype(jnp.bfloat16)
        swap(0, part, part_in, mate)
        half_out[...] = (
            part[mine, :].astype(jnp.float32) + part_in[mine, :].astype(jnp.float32)
        ).astype(jnp.bfloat16)
        swap(1, half_out, half_in, across)
        summed[mine, :] = half_out[...].astype(jnp.float32) + half_in[...].astype(jnp.float32)
        swap(2, summed.at[mine, :], summed.at[mine, :], mate)

    early[...] = jnp.zeros_like(early)

    def add_early(index, carry):
        for slot in range(1, n - 2):
            rows_in(slot, index).wait_recv()
        block = columns(index, 0, n - 2)
        for start in (0, first // 2):
            early[start : start + first // 2, :] += transposed_dot(
                block[start : start + first // 2], block
            )
        return carry

    lax.fori_loop(0, chunks, add_early, 0)
    tensor_sum(early, early_part, early_in, early_half, early_half_in, early_sum, 0)

    late[...] = jnp.zeros_like(late)

    def add_late(index, carry):
        for slot in (n - 2, n - 1):
            rows_in(slot, index).wait_recv()
        late[...] += transposed_dot(columns(index, n - 2, 2), columns(index, 0, n))
        return carry

    lax.fori_loop(0, chunks, add_late, 0)
    tensor_sum(late, late_part, late_in, late_half, late_half_in, late_sum, 3)

    def diagonal(height, width, start):
        row = start + lax.broadcasted_iota(jnp.int32, (height, width), 0)
        return row == lax.broadcasted_iota(jnp.int32, (height, width), 1)

    def trace(value, start):
        return jnp.sum(jnp.where(diagonal(*value.shape, start), value, 0.0), keepdims=True)

    squares = trace(early_sum[...], 0) + trace(late_sum[...], first)
    inv_norm = 1.0 / (jnp.sqrt(squares) + norm_epsilon)
    square_scale = inv_norm * inv_norm
    gram[:first, :first] = early_sum[...] * square_scale
    gram[first:, :] = late_sum[...] * square_scale
    gram[:first, first:] = late_sum[:, :first].T * square_scale

    strips = [(start, slice(start, start + half)) for start in (0, half)]

    def as_left(target, strip, value):
        high, low = halves(value)
        target[strip, 0:size] = high
        target[strip, size : 2 * size] = high
        target[strip, 2 * size :] = low

    def as_right(target, start, value):
        high, low = halves(value)
        target[start : start + half, :] = high
        target[size + start : size + start + half, :] = low
        target[2 * size + start : 2 * size + start + half, :] = high

    for start, strip in strips:
        as_left(gram_left, strip, gram[strip, :])
        as_right(gram_right, start, gram[strip, :])

    for step in range(ITERS):
        last = step + 1 == ITERS
        for start, strip in strips:
            factor = quintic_second * gram[strip, :] + quintic_third * narrow_dot(
                gram_left[strip, :], gram_right[...]
            )
            factor += jnp.where(diagonal(half, size, start), quintic_first, 0.0)
            as_left(fac_left, strip, factor)
            if step == 0:
                as_right(all_right, start, factor)
        if not last:
            for start, strip in strips:
                mixed[strip, :] = narrow_dot(
                    fac_left[strip, :size], gram_right[:size, :]
                ).astype(jnp.bfloat16)
            for start, strip in strips:
                following = narrow_dot(mixed[strip, :], fac_left[:, :size])
                gram[strip, :] = following
                as_left(gram_left, strip, following)
                as_right(gram_right, start, following)
        if 0 < step and not last:
            for start, strip in strips:
                passing[strip, :] = narrow_dot(fac_left[strip, :], all_right[...])
            for start, strip in strips:
                as_right(all_right, start, passing[strip, :])

    def rows_out(slot, index):
        return pltpu.make_async_remote_copy(
            src_ref=upd.at[slot * rows : (slot + 1) * rows, lanes_of(index)],
            dst_ref=ret_ref.at[me, :, lanes_of(index)],
            send_sem=out_send.at[slot, index],
            recv_sem=out_recv.at[me, index],
            device_id=(holder(slot), lane),
            device_id_type=MESH,
        )

    def write(slot):
        place = pl.ds(pl.multiple_of(holder(slot) * rows, rows), rows)
        return pltpu.make_async_copy(
            upd.at[slot * rows : (slot + 1) * rows, :], upd_ref.at[place, :], write_sem.at[slot]
        )

    for start, strip in strips:
        high, low = halves(
            narrow_dot(fac_left[strip, :], all_right[...]) * (scale_out * inv_norm)
        )
        mixed[strip, :] = high
        fac_left[strip, :size] = low

    def apply_chunk(index, carry):
        block = columns(index, 0, n)
        for start, strip in strips:
            upd[strip, lanes_of(index)] = (
                narrow_dot(mixed[strip, :], block) + narrow_dot(fac_left[strip, :size], block)
            ).astype(jnp.bfloat16)
            for slot in range(start // rows, (start + half) // rows):
                if slot:
                    rows_out(slot, index).start()
        return carry

    lax.fori_loop(0, chunks, apply_chunk, 0)
    own = pltpu.make_async_copy(upd.at[0:rows, :], ret_ref.at[me], own_sem.at[0])
    own.start()
    for slot in range(n):
        write(slot).start()

    for slot in range(1, n):
        for index in range(chunks):
            rows_in(slot, index).wait_send()
    own.wait()
    for slot in range(n):
        write(slot).wait()
    for slot in range(1, n):
        source = lax.rem(me + slot, n)
        for index in range(chunks):
            rows_out(slot, index).wait_send()
            pltpu.make_async_remote_copy(
                src_ref=upd.at[0:rows, lanes_of(index)],
                dst_ref=ret_ref.at[source, :, lanes_of(index)],
                send_sem=out_send.at[slot, index],
                recv_sem=out_recv.at[source, index],
                device_id=(source, lane),
                device_id_type=MESH,
            ).wait_recv()


def owner_call(scale_out, n, momentum, owner_order):
    rows, cols = momentum.shape[1:]
    size, first, strip = n * rows, (n - 2) * rows, 2 * rows

    def wide(*shape):
        return pltpu.VMEM(shape, jnp.float32)

    def narrow(*shape):
        return pltpu.VMEM(shape, jnp.bfloat16)

    def gram_buffers(height, width):
        return [
            wide(height, width), narrow(height, width), narrow(height, width),
            narrow(height // 2, width), narrow(height // 2, width), wide(height, width),
        ]

    dma = pltpu.SemaphoreType.DMA
    return pl.pallas_call(
        functools.partial(owner_kernel, n, rows, cols, cols // 4, scale_out),
        out_shape=(
            jax.ShapeDtypeStruct((n, rows, cols), jnp.bfloat16),
            jax.ShapeDtypeStruct((size, cols), jnp.bfloat16),
        ),
        in_specs=[
            pl.BlockSpec(memory_space=pltpu.SMEM),
            pl.BlockSpec(memory_space=pltpu.VMEM),
        ],
        out_specs=(pl.BlockSpec(memory_space=pl.ANY), pl.BlockSpec(memory_space=pl.ANY)),
        scratch_shapes=[
            narrow(n, rows, cols), narrow(n, rows, cols), narrow(size, cols), wide(size, size),
            *gram_buffers(first, first),
            *gram_buffers(strip, size),
            narrow(size, 3 * size), narrow(3 * size, size), narrow(size, 3 * size),
            narrow(3 * size, size), wide(size, size), narrow(size, size),
            dma((n, 4)), dma((n, 4)), dma((6,)), dma((6,)),
            dma((n, 4)), dma((n, 4)), dma((1,)), dma((n,)),
        ],
        compiler_params=pltpu.CompilerParams(
            collective_id=0, has_side_effects=True, vmem_limit_bytes=32 << 20
        ),
        cost_estimate=pl.CostEstimate(
            flops=6 * size * size * cols + 40 * size**3,
            bytes_accessed=12 * size * cols,
            transcendentals=0,
        ),
    )(owner_order, momentum)


def master_kernel(n, order_ref, ret_ref, upd_ref, master_ref, out_ref, upd_out_ref, fresh, sems):
    whole = pltpu.make_async_copy(upd_ref, upd_out_ref, sems.at[n])
    copies = []
    for slot in range(n):
        matrix = order_ref[slot]
        fresh[slot] = master_ref[matrix] * (1.0 - learn_rate * weight_decay) - learn_rate * ret_ref[
            slot
        ].astype(jnp.float32)
        copies.append(pltpu.make_async_copy(fresh.at[slot], out_ref.at[matrix], sems.at[slot]))
        copies[-1].start()
        if slot == 0:
            whole.start()
    for copy in copies + [whole]:
        copy.wait()


def master_call(returned, update, master, owner_order):
    n = master.shape[0]
    vmem = pl.BlockSpec(memory_space=pltpu.VMEM)
    hbm = pl.BlockSpec(memory_space=pl.ANY)
    return pl.pallas_call(
        functools.partial(master_kernel, n),
        out_shape=(
            jax.ShapeDtypeStruct(master.shape, jnp.float32),
            jax.ShapeDtypeStruct(update.shape, update.dtype),
        ),
        in_specs=[pl.BlockSpec(memory_space=pltpu.SMEM), vmem, vmem, vmem],
        out_specs=(hbm, hbm),
        scratch_shapes=[
            pltpu.VMEM(master.shape, jnp.float32), pltpu.SemaphoreType.DMA((n + 1,))
        ],
        compiler_params=pltpu.CompilerParams(vmem_limit_bytes=24 << 20),
    )(owner_order, returned, update, master)


def kernel_shards(scale_out, n, momentum, master, owner_order):
    returned, owned_update = owner_call(scale_out, n, momentum, owner_order)
    new_master, owned_update = master_call(returned, owned_update, master, owner_order)
    return new_master, owned_update[None]


def wide_dot(left, right):
    return jnp.dot(left, right, precision=lax.Precision.HIGH)


def polynomial(gram):
    eye = jnp.eye(gram.shape[0], dtype=jnp.float32)
    whole = None
    for step in range(ITERS):
        factor = (
            quintic_first * eye + quintic_second * gram + quintic_third * wide_dot(gram, gram)
        )
        whole = factor if whole is None else wide_dot(factor, whole)
        if step + 1 < ITERS:
            gram = wide_dot(wide_dot(factor, gram), factor)
    return whole


def plain_shards(scale_out, momentum, master, owner_order):
    matrices = momentum.shape[0]
    slotted = jnp.take(momentum, owner_order, axis=0)
    owned = lax.all_to_all(slotted, "dp", split_axis=0, concat_axis=1, tiled=True)

    def one(matrix):
        squares = lax.psum(jnp.sum(jnp.square(matrix.astype(jnp.float32))), "tensor")
        inv_norm = 1.0 / (jnp.sqrt(squares) + norm_epsilon)
        partial_value = lax.dot_general(
            matrix, matrix, (((1,), (1,)), ((), ())), preferred_element_type=jnp.float32
        )
        gram = lax.psum(partial_value.astype(jnp.bfloat16), "tensor").astype(jnp.float32)
        whole = polynomial(gram * (inv_norm * inv_norm)) * (scale_out * inv_norm)
        return wide_dot(whole, matrix.astype(jnp.float32)).astype(jnp.bfloat16)

    owned_update = jnp.stack([one(owned[index]) for index in range(owned.shape[0])])
    returned = lax.all_to_all(owned_update, "dp", split_axis=1, concat_axis=0, tiled=True)
    inverse = (
        jnp.zeros((matrices,), jnp.int32).at[owner_order].set(jnp.arange(matrices, dtype=jnp.int32))
    )
    by_matrix = jnp.take(returned, inverse, axis=0)
    new_master = master * (1.0 - learn_rate * weight_decay) - learn_rate * by_matrix.astype(
        jnp.float32
    )
    return (new_master, owned_update)


def solution(mesh):
    n, lanes = mesh.shape["dp"], mesh.shape["tensor"]

    def whole_call(momentum, master, owner_order):
        scale_out = 0.2 * math.sqrt(max(momentum.shape[1], momentum.shape[2]))

        def shards(momentum, master, owner_order):
            matrices, rows, cols = momentum.shape
            if matrices == n and lanes == 4 and n >= 8 and n % 4 == 0 and rows % 64 == 0 and cols % 512 == 0:
                return kernel_shards(scale_out, n, momentum, master, owner_order)
            return plain_shards(scale_out, momentum, master, owner_order)

        return jax.shard_map(
            shards,
            mesh=mesh,
            in_specs=(P(None, "dp", "tensor"), P(None, "dp", "tensor"), P()),
            out_specs=(P(None, "dp", "tensor"), P("dp", None, "tensor")),
            check_vma=False,
        )(momentum, master, owner_order)

    return whole_call
```

```python
import functools
import math

import jax
import jax.numpy as jnp
from jax import lax
from jax.experimental import pallas as pl
from jax.experimental.pallas import tpu as pltpu
from jax.sharding import PartitionSpec as P

learn_rate = 0.02
weight_decay = 0.1
norm_epsilon = 1e-07
quintic_first = 3.4445
quintic_second = -4.775
quintic_third = 2.0315
ITERS = 3
MESH = pl.DeviceIdType.MESH


def halves(value):
    high = value.astype(jnp.bfloat16)
    low = (value - high.astype(jnp.float32)).astype(jnp.bfloat16)
    return high, low


def narrow_dot(left, right):
    return jnp.dot(left, right, preferred_element_type=jnp.float32)


def transposed_dot(left, right):
    return lax.dot_general(
        left, right, (((1,), (1,)), ((), ())), preferred_element_type=jnp.float32
    )


def visit_order(n):
    last = [n - 2, 2]
    near = [n - 1, 1]
    rest = [offset for offset in range(1, n) if offset not in last + near]
    return sorted(rest, key=lambda offset: (abs(offset - n // 2), offset)) + near + last


def owner_kernel(
    n, rows, cols, chunk, scale_out,
    order_ref, mom_ref, ret_ref, upd_ref,
    send, recv, upd, gram,
    early, early_part, early_in, early_half, early_half_in, early_sum,
    late, late_part, late_in, late_half, late_half_in, late_sum,
    mixed, fac, fac_first, pair_hi, pair_lo, whole_hi, whole_lo,
    in_send, in_recv, sum_send, sum_recv, out_send, out_recv, own_sem, write_sem,
):
    me = lax.axis_index("dp")
    lane = lax.axis_index("tensor")
    core = lax.rem(lane, 2)
    mate = lane + 1 - 2 * core
    across = lax.rem(lane + 2, 4)
    size = n * rows
    half = size // 2
    first = size - 2 * rows
    chunks = cols // chunk
    order = visit_order(n)

    barrier = pltpu.get_barrier_semaphore()
    for offset in range(1, n):
        pl.semaphore_signal(
            barrier, inc=1, device_id=(lax.rem(me + offset, n), lane), device_id_type=MESH
        )
    for other in (mate, across):
        pl.semaphore_signal(barrier, inc=1, device_id=(me, other), device_id_type=MESH)
    pl.semaphore_wait(barrier, n + 1)

    def rows_in(slot):
        return pltpu.make_async_remote_copy(
            src_ref=send.at[slot],
            dst_ref=recv.at[slot],
            send_sem=in_send.at[slot],
            recv_sem=in_recv.at[slot],
            device_id=(lax.rem(me + order[slot - 1], n), lane),
            device_id_type=MESH,
        )

    def holder(slot):
        return lax.rem(me + n - order[slot - 1], n) if slot else me

    for slot in range(1, n):
        send[slot] = mom_ref[order_ref[lax.rem(me + order[slot - 1], n)]]
        rows_in(slot).start()
    recv[0] = mom_ref[order_ref[me]]

    def columns(index, start, count):
        place = pl.ds(pl.multiple_of(index * chunk, chunk), chunk)
        return recv[start : start + count, :, place].reshape(count * rows, chunk)

    def tensor_sum(total, part, part_in, half_out, half_in, summed, sem):
        count = total.shape[0] // 2
        mine = pl.ds(pl.multiple_of(core * count, count), count)

        def swap(step, source, target, other):
            copy = pltpu.make_async_remote_copy(
                src_ref=source, dst_ref=target,
                send_sem=sum_send.at[sem + step], recv_sem=sum_recv.at[sem + step],
                device_id=(me, other), device_id_type=MESH,
            )
            copy.start()
            copy.wait()

        part[...] = total[...].astype(jnp.bfloat16)
        swap(0, part, part_in, mate)
        half_out[...] = (
            part[mine, :].astype(jnp.float32) + part_in[mine, :].astype(jnp.float32)
        ).astype(jnp.bfloat16)
        swap(1, half_out, half_in, across)
        summed[mine, :] = half_out[...].astype(jnp.float32) + half_in[...].astype(jnp.float32)
        swap(2, summed.at[mine, :], summed.at[mine, :], mate)

    for slot in range(1, n - 2):
        rows_in(slot).wait_recv()
    early[...] = jnp.zeros_like(early)

    def add_early(index, carry):
        block = columns(index, 0, n - 2)
        for start in (0, first // 2):
            early[start : start + first // 2, :] += transposed_dot(
                block[start : start + first // 2], block
            )
        return carry

    lax.fori_loop(0, chunks, add_early, 0)
    tensor_sum(early, early_part, early_in, early_half, early_half_in, early_sum, 0)

    for slot in (n - 2, n - 1):
        rows_in(slot).wait_recv()
    late[...] = jnp.zeros_like(late)

    def add_late(index, carry):
        late[...] += transposed_dot(columns(index, n - 2, 2), columns(index, 0, n))
        return carry

    lax.fori_loop(0, chunks, add_late, 0)
    tensor_sum(late, late_part, late_in, late_half, late_half_in, late_sum, 3)

    def diagonal(height, width, start):
        row = start + lax.broadcasted_iota(jnp.int32, (height, width), 0)
        return row == lax.broadcasted_iota(jnp.int32, (height, width), 1)

    def trace(value, start):
        return jnp.sum(jnp.where(diagonal(*value.shape, start), value, 0.0), keepdims=True)

    squares = trace(early_sum[...], 0) + trace(late_sum[...], first)
    inv_norm = 1.0 / (jnp.sqrt(squares) + norm_epsilon)
    square_scale = inv_norm * inv_norm
    gram[:first, :first] = (early_sum[...] * square_scale).astype(jnp.bfloat16)
    gram[first:, :] = (late_sum[...] * square_scale).astype(jnp.bfloat16)
    gram[:first, first:] = (late_sum[:, :first].T * square_scale).astype(jnp.bfloat16)

    strips = [(start, slice(start, start + half)) for start in (0, half)]
    for step in range(ITERS):
        for start, strip in strips:
            factor = quintic_second * gram[strip, :].astype(jnp.float32)
            factor += quintic_third * narrow_dot(gram[strip, :], gram[...])
            factor += jnp.where(diagonal(half, size, start), quintic_first, 0.0)
            fac[strip, :] = factor.astype(jnp.bfloat16)
        if step + 1 < ITERS:
            for start, strip in strips:
                mixed[strip, :] = narrow_dot(fac[strip, :], gram[...]).astype(jnp.bfloat16)
            for start, strip in strips:
                gram[strip, :] = narrow_dot(mixed[strip, :], fac[...]).astype(jnp.bfloat16)
        if step == 0:
            fac_first[...] = fac[...]
        elif step == 1:
            for start, strip in strips:
                pair_hi[strip, :], pair_lo[strip, :] = halves(
                    narrow_dot(fac[strip, :], fac_first[...])
                )

    def rows_out(slot):
        return pltpu.make_async_remote_copy(
            src_ref=upd.at[slot * rows : (slot + 1) * rows, :],
            dst_ref=ret_ref.at[me],
            send_sem=out_send.at[slot],
            recv_sem=out_recv.at[me],
            device_id=(holder(slot), lane),
            device_id_type=MESH,
        )

    def write(slot):
        place = pl.ds(pl.multiple_of(holder(slot) * rows, rows), rows)
        return pltpu.make_async_copy(
            upd.at[slot * rows : (slot + 1) * rows, :], upd_ref.at[place, :], write_sem.at[slot]
        )

    own = pltpu.make_async_copy(upd.at[0:rows, :], ret_ref.at[me], own_sem.at[0])
    for start, strip in strips:
        high, low = halves(
            (narrow_dot(fac[strip, :], pair_hi[...]) + narrow_dot(fac[strip, :], pair_lo[...]))
            * (scale_out * inv_norm)
        )
        whole_hi[strip, :] = high
        whole_lo[strip, :] = low
        for top in range(start, start + half, 2 * rows):

            def apply_chunk(index, carry, top=top):
                place = pl.ds(pl.multiple_of(index * chunk, chunk), chunk)
                block = columns(index, 0, n)
                upd[top : top + 2 * rows, place] = (
                    narrow_dot(whole_hi[top : top + 2 * rows, :], block)
                    + narrow_dot(whole_lo[top : top + 2 * rows, :], block)
                ).astype(jnp.bfloat16)
                return carry

            lax.fori_loop(0, chunks, apply_chunk, 0)
            for slot in (top // rows, top // rows + 1):
                if slot:
                    rows_out(slot).start()
                else:
                    own.start()
    for slot in range(n):
        write(slot).start()

    for slot in range(1, n):
        rows_in(slot).wait_send()
    own.wait()
    for slot in range(n):
        write(slot).wait()
    for slot in range(1, n):
        rows_out(slot).wait_send()
        source = lax.rem(me + slot, n)
        pltpu.make_async_remote_copy(
            src_ref=upd.at[0:rows, :],
            dst_ref=ret_ref.at[source],
            send_sem=out_send.at[slot],
            recv_sem=out_recv.at[source],
            device_id=(source, lane),
            device_id_type=MESH,
        ).wait_recv()


def owner_call(scale_out, n, momentum, owner_order):
    rows, cols = momentum.shape[1:]
    size, first, strip = n * rows, (n - 2) * rows, 2 * rows

    def wide(*shape):
        return pltpu.VMEM(shape, jnp.float32)

    def narrow(*shape):
        return pltpu.VMEM(shape, jnp.bfloat16)

    def gram_buffers(height, width):
        return [
            wide(height, width), narrow(height, width), narrow(height, width),
            narrow(height // 2, width), narrow(height // 2, width), wide(height, width),
        ]

    dma = pltpu.SemaphoreType.DMA
    return pl.pallas_call(
        functools.partial(owner_kernel, n, rows, cols, cols // 4, scale_out),
        out_shape=(
            jax.ShapeDtypeStruct((n, rows, cols), jnp.bfloat16),
            jax.ShapeDtypeStruct((size, cols), jnp.bfloat16),
        ),
        in_specs=[
            pl.BlockSpec(memory_space=pltpu.SMEM),
            pl.BlockSpec(memory_space=pltpu.VMEM),
        ],
        out_specs=(pl.BlockSpec(memory_space=pl.ANY), pl.BlockSpec(memory_space=pl.ANY)),
        scratch_shapes=[
            narrow(n, rows, cols), narrow(n, rows, cols), narrow(size, cols), narrow(size, size),
            *gram_buffers(first, first),
            *gram_buffers(strip, size),
            *[narrow(size, size)] * 7,
            dma((n,)), dma((n,)), dma((6,)), dma((6,)), dma((n,)), dma((n,)), dma((1,)), dma((n,)),
        ],
        compiler_params=pltpu.CompilerParams(
            collective_id=0, has_side_effects=True, vmem_limit_bytes=32 << 20
        ),
        cost_estimate=pl.CostEstimate(
            flops=6 * size * size * cols + 40 * size**3,
            bytes_accessed=12 * size * cols,
            transcendentals=0,
        ),
    )(owner_order, momentum)


def master_kernel(n, order_ref, ret_ref, upd_ref, master_ref, out_ref, upd_out_ref, fresh, sems):
    whole = pltpu.make_async_copy(upd_ref, upd_out_ref, sems.at[n])
    copies = []
    for slot in range(n):
        matrix = order_ref[slot]
        fresh[slot] = master_ref[matrix] * (1.0 - learn_rate * weight_decay) - learn_rate * ret_ref[
            slot
        ].astype(jnp.float32)
        copies.append(pltpu.make_async_copy(fresh.at[slot], out_ref.at[matrix], sems.at[slot]))
        copies[-1].start()
        if slot == 0:
            whole.start()
    for copy in copies + [whole]:
        copy.wait()


def master_call(returned, update, master, owner_order):
    n = master.shape[0]
    vmem = pl.BlockSpec(memory_space=pltpu.VMEM)
    hbm = pl.BlockSpec(memory_space=pl.ANY)
    return pl.pallas_call(
        functools.partial(master_kernel, n),
        out_shape=(
            jax.ShapeDtypeStruct(master.shape, jnp.float32),
            jax.ShapeDtypeStruct(update.shape, update.dtype),
        ),
        in_specs=[pl.BlockSpec(memory_space=pltpu.SMEM), vmem, vmem, vmem],
        out_specs=(hbm, hbm),
        scratch_shapes=[
            pltpu.VMEM(master.shape, jnp.float32), pltpu.SemaphoreType.DMA((n + 1,))
        ],
        compiler_params=pltpu.CompilerParams(vmem_limit_bytes=24 << 20),
    )(owner_order, returned, update, master)


def kernel_shards(scale_out, n, momentum, master, owner_order):
    returned, owned_update = owner_call(scale_out, n, momentum, owner_order)
    new_master, owned_update = master_call(returned, owned_update, master, owner_order)
    return new_master, owned_update[None]


def wide_dot(left, right):
    return jnp.dot(left, right, precision=lax.Precision.HIGH)


def polynomial(gram):
    eye = jnp.eye(gram.shape[0], dtype=jnp.float32)
    whole = None
    for step in range(ITERS):
        factor = (
            quintic_first * eye + quintic_second * gram + quintic_third * wide_dot(gram, gram)
        )
        whole = factor if whole is None else wide_dot(factor, whole)
        if step + 1 < ITERS:
            gram = wide_dot(wide_dot(factor, gram), factor)
    return whole


def plain_shards(scale_out, momentum, master, owner_order):
    matrices = momentum.shape[0]
    slotted = jnp.take(momentum, owner_order, axis=0)
    owned = lax.all_to_all(slotted, "dp", split_axis=0, concat_axis=1, tiled=True)

    def one(matrix):
        squares = lax.psum(jnp.sum(jnp.square(matrix.astype(jnp.float32))), "tensor")
        inv_norm = 1.0 / (jnp.sqrt(squares) + norm_epsilon)
        partial_value = lax.dot_general(
            matrix, matrix, (((1,), (1,)), ((), ())), preferred_element_type=jnp.float32
        )
        gram = lax.psum(partial_value.astype(jnp.bfloat16), "tensor").astype(jnp.float32)
        whole = polynomial(gram * (inv_norm * inv_norm)) * (scale_out * inv_norm)
        return wide_dot(whole, matrix.astype(jnp.float32)).astype(jnp.bfloat16)

    owned_update = jnp.stack([one(owned[index]) for index in range(owned.shape[0])])
    returned = lax.all_to_all(owned_update, "dp", split_axis=1, concat_axis=0, tiled=True)
    inverse = (
        jnp.zeros((matrices,), jnp.int32).at[owner_order].set(jnp.arange(matrices, dtype=jnp.int32))
    )
    by_matrix = jnp.take(returned, inverse, axis=0)
    new_master = master * (1.0 - learn_rate * weight_decay) - learn_rate * by_matrix.astype(
        jnp.float32
    )
    return (new_master, owned_update)


def solution(mesh):
    n, lanes = mesh.shape["dp"], mesh.shape["tensor"]

    def whole_call(momentum, master, owner_order):
        scale_out = 0.2 * math.sqrt(max(momentum.shape[1], momentum.shape[2]))

        def shards(momentum, master, owner_order):
            matrices, rows, cols = momentum.shape
            if matrices == n and lanes == 4 and n >= 8 and n % 4 == 0 and rows % 64 == 0 and cols % 512 == 0:
                return kernel_shards(scale_out, n, momentum, master, owner_order)
            return plain_shards(scale_out, momentum, master, owner_order)

        return jax.shard_map(
            shards,
            mesh=mesh,
            in_specs=(P(None, "dp", "tensor"), P(None, "dp", "tensor"), P()),
            out_specs=(P(None, "dp", "tensor"), P("dp", None, "tensor")),
            check_vma=False,
        )(momentum, master, owner_order)

    return whole_call
```

```python
import functools
import math

import jax
import jax.numpy as jnp
from jax import lax
from jax.experimental import pallas as pl
from jax.experimental.pallas import tpu as pltpu
from jax.sharding import PartitionSpec as P

learn_rate = 0.02
weight_decay = 0.1
norm_epsilon = 1e-07
quintic_first = 3.4445
quintic_second = -4.775
quintic_third = 2.0315
ITERS = 3
MESH = pl.DeviceIdType.MESH


def halves(value):
    high = value.astype(jnp.bfloat16)
    low = (value - high.astype(jnp.float32)).astype(jnp.bfloat16)
    return high, low


def narrow_dot(left, right):
    return jnp.dot(left, right, preferred_element_type=jnp.float32)


def transposed_dot(left, right):
    return lax.dot_general(
        left, right, (((1,), (1,)), ((), ())), preferred_element_type=jnp.float32
    )


def visit_shifts(n):
    shifts = [(pair, bit) for pair in range(1, n // 2) for bit in (0, 1)]
    return shifts[:2] + [(0, 1)] + shifts[2:]


def owner_kernel(
    n, rows, cols, chunk, scale_out,
    order_ref, mom_ref, ret_ref, upd_ref,
    send, recv, upd, gram,
    early, early_part, early_in, early_half, early_half_in, early_sum,
    late, late_part, late_in, late_half, late_half_in, late_sum,
    mixed, fac, fac_first, pair_hi, pair_lo, whole_hi, whole_lo,
    in_send, in_recv, sum_send, sum_recv, out_send, out_recv, own_sem, write_sem,
):
    me = lax.axis_index("dp")
    lane = lax.axis_index("tensor")
    core = lax.rem(lane, 2)
    mate = lane + 1 - 2 * core
    across = lax.rem(lane + 2, 4)
    size = n * rows
    half = size // 2
    first = size - 2 * rows
    chunks = cols // chunk
    shifts = visit_shifts(n)
    pairs = n // 2
    pair = lax.div(me, 2)
    bit = lax.rem(me, 2)
    even = lax.rem(pair, 2) == 0

    def target(slot):
        shift = shifts[slot - 1]
        return 2 * lax.rem(pair + shift[0], pairs) + lax.rem(bit + shift[1], 2)

    def holder(slot):
        if slot == 0:
            return me
        shift = shifts[slot - 1]
        return 2 * lax.rem(pair + pairs - shift[0], pairs) + lax.rem(bit + shift[1], 2)

    def start_in_turn(slot, start):
        if slot == 3:
            pl.when(even)(lambda: start(3))
        else:
            start(slot)
        if slot == 5:
            pl.when(jnp.logical_not(even))(lambda: start(3))

    barrier = pltpu.get_barrier_semaphore()
    for offset in range(1, n):
        pl.semaphore_signal(
            barrier, inc=1, device_id=(lax.rem(me + offset, n), lane), device_id_type=MESH
        )
    for other in (mate, across):
        pl.semaphore_signal(barrier, inc=1, device_id=(me, other), device_id_type=MESH)
    pl.semaphore_wait(barrier, n + 1)

    def rows_in(slot):
        return pltpu.make_async_remote_copy(
            src_ref=send.at[slot],
            dst_ref=recv.at[slot],
            send_sem=in_send.at[slot],
            recv_sem=in_recv.at[slot],
            device_id=(target(slot), lane),
            device_id_type=MESH,
        )

    for slot in range(1, n):
        send[slot] = mom_ref[order_ref[target(slot)]]
        start_in_turn(slot, lambda slot: rows_in(slot).start())
    recv[0] = mom_ref[order_ref[me]]

    def columns(index, start, count):
        place = pl.ds(pl.multiple_of(index * chunk, chunk), chunk)
        return recv[start : start + count, :, place].reshape(count * rows, chunk)

    def tensor_sum(total, part, part_in, half_out, half_in, summed, sem):
        count = total.shape[0] // 2
        mine = pl.ds(pl.multiple_of(core * count, count), count)

        def swap(step, source, target, other):
            copy = pltpu.make_async_remote_copy(
                src_ref=source, dst_ref=target,
                send_sem=sum_send.at[sem + step], recv_sem=sum_recv.at[sem + step],
                device_id=(me, other), device_id_type=MESH,
            )
            copy.start()
            copy.wait()

        part[...] = total[...].astype(jnp.bfloat16)
        swap(0, part, part_in, mate)
        half_out[...] = (
            part[mine, :].astype(jnp.float32) + part_in[mine, :].astype(jnp.float32)
        ).astype(jnp.bfloat16)
        swap(1, half_out, half_in, across)
        summed[mine, :] = half_out[...].astype(jnp.float32) + half_in[...].astype(jnp.float32)
        swap(2, summed.at[mine, :], summed.at[mine, :], mate)

    for slot in range(1, n - 2):
        rows_in(slot).wait_recv()
    early[...] = jnp.zeros_like(early)

    def add_early(index, carry):
        block = columns(index, 0, n - 2)
        for start in (0, first // 2):
            early[start : start + first // 2, :] += transposed_dot(
                block[start : start + first // 2], block
            )
        return carry

    lax.fori_loop(0, chunks, add_early, 0)
    tensor_sum(early, early_part, early_in, early_half, early_half_in, early_sum, 0)

    for slot in (n - 2, n - 1):
        rows_in(slot).wait_recv()
    late[...] = jnp.zeros_like(late)

    def add_late(index, carry):
        late[...] += transposed_dot(columns(index, n - 2, 2), columns(index, 0, n))
        return carry

    lax.fori_loop(0, chunks, add_late, 0)
    tensor_sum(late, late_part, late_in, late_half, late_half_in, late_sum, 3)

    def diagonal(height, width, start):
        row = start + lax.broadcasted_iota(jnp.int32, (height, width), 0)
        return row == lax.broadcasted_iota(jnp.int32, (height, width), 1)

    def trace(value, start):
        return jnp.sum(jnp.where(diagonal(*value.shape, start), value, 0.0), keepdims=True)

    squares = trace(early_sum[...], 0) + trace(late_sum[...], first)
    inv_norm = 1.0 / (jnp.sqrt(squares) + norm_epsilon)
    square_scale = inv_norm * inv_norm
    gram[:first, :first] = (early_sum[...] * square_scale).astype(jnp.bfloat16)
    gram[first:, :] = (late_sum[...] * square_scale).astype(jnp.bfloat16)
    gram[:first, first:] = (late_sum[:, :first].T * square_scale).astype(jnp.bfloat16)

    strips = [(start, slice(start, start + half)) for start in (0, half)]
    for step in range(ITERS):
        for start, strip in strips:
            factor = quintic_second * gram[strip, :].astype(jnp.float32)
            factor += quintic_third * narrow_dot(gram[strip, :], gram[...])
            factor += jnp.where(diagonal(half, size, start), quintic_first, 0.0)
            fac[strip, :] = factor.astype(jnp.bfloat16)
        if step + 1 < ITERS:
            for start, strip in strips:
                mixed[strip, :] = narrow_dot(fac[strip, :], gram[...]).astype(jnp.bfloat16)
            for start, strip in strips:
                gram[strip, :] = narrow_dot(mixed[strip, :], fac[...]).astype(jnp.bfloat16)
        if step == 0:
            fac_first[...] = fac[...]
        elif step == 1:
            for start, strip in strips:
                pair_hi[strip, :], pair_lo[strip, :] = halves(
                    narrow_dot(fac[strip, :], fac_first[...])
                )

    def rows_out(slot):
        return pltpu.make_async_remote_copy(
            src_ref=upd.at[slot * rows : (slot + 1) * rows, :],
            dst_ref=ret_ref.at[me],
            send_sem=out_send.at[slot],
            recv_sem=out_recv.at[me],
            device_id=(holder(slot), lane),
            device_id_type=MESH,
        )

    def write(slot):
        place = pl.ds(pl.multiple_of(holder(slot) * rows, rows), rows)
        return pltpu.make_async_copy(
            upd.at[slot * rows : (slot + 1) * rows, :], upd_ref.at[place, :], write_sem.at[slot]
        )

    own = pltpu.make_async_copy(upd.at[0:rows, :], ret_ref.at[me], own_sem.at[0])
    for start, strip in strips:
        high, low = halves(
            (narrow_dot(fac[strip, :], pair_hi[...]) + narrow_dot(fac[strip, :], pair_lo[...]))
            * (scale_out * inv_norm)
        )
        whole_hi[strip, :] = high
        whole_lo[strip, :] = low
        for top in range(start, start + half, 2 * rows):

            def apply_chunk(index, carry, top=top):
                place = pl.ds(pl.multiple_of(index * chunk, chunk), chunk)
                block = columns(index, 0, n)
                upd[top : top + 2 * rows, place] = (
                    narrow_dot(whole_hi[top : top + 2 * rows, :], block)
                    + narrow_dot(whole_lo[top : top + 2 * rows, :], block)
                ).astype(jnp.bfloat16)
                return carry

            lax.fori_loop(0, chunks, apply_chunk, 0)
            for slot in (top // rows, top // rows + 1):
                if slot:
                    start_in_turn(slot, lambda slot: rows_out(slot).start())
                else:
                    own.start()
    for slot in range(n):
        write(slot).start()

    for slot in range(1, n):
        rows_in(slot).wait_send()
    own.wait()
    for slot in range(n):
        write(slot).wait()
    for slot in range(1, n):
        rows_out(slot).wait_send()
        source = lax.rem(me + slot, n)
        pltpu.make_async_remote_copy(
            src_ref=upd.at[0:rows, :],
            dst_ref=ret_ref.at[source],
            send_sem=out_send.at[slot],
            recv_sem=out_recv.at[source],
            device_id=(source, lane),
            device_id_type=MESH,
        ).wait_recv()


def owner_call(scale_out, n, momentum, owner_order):
    rows, cols = momentum.shape[1:]
    size, first, strip = n * rows, (n - 2) * rows, 2 * rows

    def wide(*shape):
        return pltpu.VMEM(shape, jnp.float32)

    def narrow(*shape):
        return pltpu.VMEM(shape, jnp.bfloat16)

    def gram_buffers(height, width):
        return [
            wide(height, width), narrow(height, width), narrow(height, width),
            narrow(height // 2, width), narrow(height // 2, width), wide(height, width),
        ]

    dma = pltpu.SemaphoreType.DMA
    return pl.pallas_call(
        functools.partial(owner_kernel, n, rows, cols, cols // 4, scale_out),
        out_shape=(
            jax.ShapeDtypeStruct((n, rows, cols), jnp.bfloat16),
            jax.ShapeDtypeStruct((size, cols), jnp.bfloat16),
        ),
        in_specs=[
            pl.BlockSpec(memory_space=pltpu.SMEM),
            pl.BlockSpec(memory_space=pltpu.VMEM),
        ],
        out_specs=(pl.BlockSpec(memory_space=pl.ANY), pl.BlockSpec(memory_space=pl.ANY)),
        scratch_shapes=[
            narrow(n, rows, cols), narrow(n, rows, cols), narrow(size, cols), narrow(size, size),
            *gram_buffers(first, first),
            *gram_buffers(strip, size),
            *[narrow(size, size)] * 7,
            dma((n,)), dma((n,)), dma((6,)), dma((6,)), dma((n,)), dma((n,)), dma((1,)), dma((n,)),
        ],
        compiler_params=pltpu.CompilerParams(
            collective_id=0, has_side_effects=True, vmem_limit_bytes=32 << 20
        ),
        cost_estimate=pl.CostEstimate(
            flops=6 * size * size * cols + 40 * size**3,
            bytes_accessed=12 * size * cols,
            transcendentals=0,
        ),
    )(owner_order, momentum)


def master_kernel(n, order_ref, ret_ref, upd_ref, master_ref, out_ref, upd_out_ref, fresh, sems):
    whole = pltpu.make_async_copy(upd_ref, upd_out_ref, sems.at[n])
    copies = []
    for slot in range(n):
        matrix = order_ref[slot]
        fresh[slot] = master_ref[matrix] * (1.0 - learn_rate * weight_decay) - learn_rate * ret_ref[
            slot
        ].astype(jnp.float32)
        copies.append(pltpu.make_async_copy(fresh.at[slot], out_ref.at[matrix], sems.at[slot]))
        copies[-1].start()
        if slot == 0:
            whole.start()
    for copy in copies + [whole]:
        copy.wait()


def master_call(returned, update, master, owner_order):
    n = master.shape[0]
    vmem = pl.BlockSpec(memory_space=pltpu.VMEM)
    hbm = pl.BlockSpec(memory_space=pl.ANY)
    return pl.pallas_call(
        functools.partial(master_kernel, n),
        out_shape=(
            jax.ShapeDtypeStruct(master.shape, jnp.float32),
            jax.ShapeDtypeStruct(update.shape, update.dtype),
        ),
        in_specs=[pl.BlockSpec(memory_space=pltpu.SMEM), vmem, vmem, vmem],
        out_specs=(hbm, hbm),
        scratch_shapes=[
            pltpu.VMEM(master.shape, jnp.float32), pltpu.SemaphoreType.DMA((n + 1,))
        ],
        compiler_params=pltpu.CompilerParams(vmem_limit_bytes=24 << 20),
    )(owner_order, returned, update, master)


def kernel_shards(scale_out, n, momentum, master, owner_order):
    returned, owned_update = owner_call(scale_out, n, momentum, owner_order)
    new_master, owned_update = master_call(returned, owned_update, master, owner_order)
    return new_master, owned_update[None]


def wide_dot(left, right):
    return jnp.dot(left, right, precision=lax.Precision.HIGH)


def polynomial(gram):
    eye = jnp.eye(gram.shape[0], dtype=jnp.float32)
    whole = None
    for step in range(ITERS):
        factor = (
            quintic_first * eye + quintic_second * gram + quintic_third * wide_dot(gram, gram)
        )
        whole = factor if whole is None else wide_dot(factor, whole)
        if step + 1 < ITERS:
            gram = wide_dot(wide_dot(factor, gram), factor)
    return whole


def plain_shards(scale_out, momentum, master, owner_order):
    matrices = momentum.shape[0]
    slotted = jnp.take(momentum, owner_order, axis=0)
    owned = lax.all_to_all(slotted, "dp", split_axis=0, concat_axis=1, tiled=True)

    def one(matrix):
        squares = lax.psum(jnp.sum(jnp.square(matrix.astype(jnp.float32))), "tensor")
        inv_norm = 1.0 / (jnp.sqrt(squares) + norm_epsilon)
        partial_value = lax.dot_general(
            matrix, matrix, (((1,), (1,)), ((), ())), preferred_element_type=jnp.float32
        )
        gram = lax.psum(partial_value.astype(jnp.bfloat16), "tensor").astype(jnp.float32)
        whole = polynomial(gram * (inv_norm * inv_norm)) * (scale_out * inv_norm)
        return wide_dot(whole, matrix.astype(jnp.float32)).astype(jnp.bfloat16)

    owned_update = jnp.stack([one(owned[index]) for index in range(owned.shape[0])])
    returned = lax.all_to_all(owned_update, "dp", split_axis=1, concat_axis=0, tiled=True)
    inverse = (
        jnp.zeros((matrices,), jnp.int32).at[owner_order].set(jnp.arange(matrices, dtype=jnp.int32))
    )
    by_matrix = jnp.take(returned, inverse, axis=0)
    new_master = master * (1.0 - learn_rate * weight_decay) - learn_rate * by_matrix.astype(
        jnp.float32
    )
    return (new_master, owned_update)


def solution(mesh):
    n, lanes = mesh.shape["dp"], mesh.shape["tensor"]

    def whole_call(momentum, master, owner_order):
        scale_out = 0.2 * math.sqrt(max(momentum.shape[1], momentum.shape[2]))

        def shards(momentum, master, owner_order):
            matrices, rows, cols = momentum.shape
            if matrices == n and lanes == 4 and n >= 8 and n % 4 == 0 and rows % 64 == 0 and cols % 512 == 0:
                return kernel_shards(scale_out, n, momentum, master, owner_order)
            return plain_shards(scale_out, momentum, master, owner_order)

        return jax.shard_map(
            shards,
            mesh=mesh,
            in_specs=(P(None, "dp", "tensor"), P(None, "dp", "tensor"), P()),
            out_specs=(P(None, "dp", "tensor"), P("dp", None, "tensor")),
            check_vma=False,
        )(momentum, master, owner_order)

    return whole_call
```

```python
import functools
import math

import jax
import jax.numpy as jnp
from jax import lax
from jax.experimental import pallas as pl
from jax.experimental.pallas import tpu as pltpu
from jax.sharding import PartitionSpec as P

learn_rate = 0.02
weight_decay = 0.1
norm_epsilon = 1e-07
quintic_first = 3.4445
quintic_second = -4.775
quintic_third = 2.0315
ITERS = 3
MESH = pl.DeviceIdType.MESH


def halves(value):
    high = value.astype(jnp.bfloat16)
    low = (value - high.astype(jnp.float32)).astype(jnp.bfloat16)
    return high, low


def narrow_dot(left, right):
    return jnp.dot(left, right, preferred_element_type=jnp.float32)


def transposed_dot(left, right):
    return lax.dot_general(
        left, right, (((1,), (1,)), ((), ())), preferred_element_type=jnp.float32
    )


def visit_shifts(n):
    middle = n // 4
    others = [pair for pair in range(1, n // 2) if pair != middle]
    shifts = [(0, 1), (middle, 0), (middle, 1)]
    return shifts + [(pair, bit) for bit in (0, 1) for pair in others]


def owner_kernel(
    n, rows, cols, chunk, scale_out,
    order_ref, mom_ref, ret_ref, upd_ref,
    send, recv, upd, gram,
    early, early_part, early_in, early_half, early_half_in, early_sum,
    late, late_part, late_in, late_half, late_half_in, late_sum,
    mixed, fac, fac_first, pair_hi, pair_lo, whole_hi, whole_lo,
    in_send, in_recv, sum_send, sum_recv, out_send, out_recv, own_sem, write_sem,
):
    me = lax.axis_index("dp")
    lane = lax.axis_index("tensor")
    core = lax.rem(lane, 2)
    mate = lane + 1 - 2 * core
    across = lax.rem(lane + 2, 4)
    size = n * rows
    half = size // 2
    first = size - 2 * rows
    chunks = cols // chunk
    shifts = visit_shifts(n)
    pairs = n // 2
    pair = lax.div(me, 2)
    bit = lax.rem(me, 2)
    even = lax.rem(pair, 2) == 0

    def target(slot):
        shift = shifts[slot - 1]
        return 2 * lax.rem(pair + shift[0], pairs) + lax.rem(bit + shift[1], 2)

    def holder(slot):
        if slot == 0:
            return me
        shift = shifts[slot - 1]
        return 2 * lax.rem(pair + pairs - shift[0], pairs) + lax.rem(bit + shift[1], 2)

    def start_in_turn(slot, start):
        if slot == 1:
            pl.when(even)(lambda: start(1))
        else:
            start(slot)
        if slot == 2:
            pl.when(jnp.logical_not(even))(lambda: start(1))

    barrier = pltpu.get_barrier_semaphore()
    for offset in range(1, n):
        pl.semaphore_signal(
            barrier, inc=1, device_id=(lax.rem(me + offset, n), lane), device_id_type=MESH
        )
    for other in (mate, across):
        pl.semaphore_signal(barrier, inc=1, device_id=(me, other), device_id_type=MESH)
    pl.semaphore_wait(barrier, n + 1)

    def rows_in(slot):
        return pltpu.make_async_remote_copy(
            src_ref=send.at[slot],
            dst_ref=recv.at[slot],
            send_sem=in_send.at[slot],
            recv_sem=in_recv.at[slot],
            device_id=(target(slot), lane),
            device_id_type=MESH,
        )

    for slot in range(1, n):
        send[slot] = mom_ref[order_ref[target(slot)]]
        start_in_turn(slot, lambda slot: rows_in(slot).start())
    recv[0] = mom_ref[order_ref[me]]

    def columns(index, start, count):
        place = pl.ds(pl.multiple_of(index * chunk, chunk), chunk)
        return recv[start : start + count, :, place].reshape(count * rows, chunk)

    def tensor_sum(total, part, part_in, half_out, half_in, summed, sem):
        count = total.shape[0] // 2
        mine = pl.ds(pl.multiple_of(core * count, count), count)

        def swap(step, source, target, other):
            copy = pltpu.make_async_remote_copy(
                src_ref=source, dst_ref=target,
                send_sem=sum_send.at[sem + step], recv_sem=sum_recv.at[sem + step],
                device_id=(me, other), device_id_type=MESH,
            )
            copy.start()
            copy.wait()

        part[...] = total[...].astype(jnp.bfloat16)
        swap(0, part, part_in, mate)
        half_out[...] = (
            part[mine, :].astype(jnp.float32) + part_in[mine, :].astype(jnp.float32)
        ).astype(jnp.bfloat16)
        swap(1, half_out, half_in, across)
        summed[mine, :] = half_out[...].astype(jnp.float32) + half_in[...].astype(jnp.float32)
        swap(2, summed.at[mine, :], summed.at[mine, :], mate)

    for slot in range(1, n - 2):
        rows_in(slot).wait_recv()
    early[...] = jnp.zeros_like(early)

    def add_early(index, carry):
        block = columns(index, 0, n - 2)
        for start in (0, first // 2):
            early[start : start + first // 2, :] += transposed_dot(
                block[start : start + first // 2], block
            )
        return carry

    lax.fori_loop(0, chunks, add_early, 0)
    tensor_sum(early, early_part, early_in, early_half, early_half_in, early_sum, 0)

    for slot in (n - 2, n - 1):
        rows_in(slot).wait_recv()
    late[...] = jnp.zeros_like(late)

    def add_late(index, carry):
        late[...] += transposed_dot(columns(index, n - 2, 2), columns(index, 0, n))
        return carry

    lax.fori_loop(0, chunks, add_late, 0)
    tensor_sum(late, late_part, late_in, late_half, late_half_in, late_sum, 3)

    def diagonal(height, width, start):
        row = start + lax.broadcasted_iota(jnp.int32, (height, width), 0)
        return row == lax.broadcasted_iota(jnp.int32, (height, width), 1)

    def trace(value, start):
        return jnp.sum(jnp.where(diagonal(*value.shape, start), value, 0.0), keepdims=True)

    squares = trace(early_sum[...], 0) + trace(late_sum[...], first)
    inv_norm = 1.0 / (jnp.sqrt(squares) + norm_epsilon)
    square_scale = inv_norm * inv_norm
    gram[:first, :first] = (early_sum[...] * square_scale).astype(jnp.bfloat16)
    gram[first:, :] = (late_sum[...] * square_scale).astype(jnp.bfloat16)
    gram[:first, first:] = (late_sum[:, :first].T * square_scale).astype(jnp.bfloat16)

    strips = [(start, slice(start, start + half)) for start in (0, half)]
    for step in range(ITERS):
        for start, strip in strips:
            factor = quintic_second * gram[strip, :].astype(jnp.float32)
            factor += quintic_third * narrow_dot(gram[strip, :], gram[...])
            factor += jnp.where(diagonal(half, size, start), quintic_first, 0.0)
            fac[strip, :] = factor.astype(jnp.bfloat16)
        if step + 1 < ITERS:
            for start, strip in strips:
                mixed[strip, :] = narrow_dot(fac[strip, :], gram[...]).astype(jnp.bfloat16)
            for start, strip in strips:
                gram[strip, :] = narrow_dot(mixed[strip, :], fac[...]).astype(jnp.bfloat16)
        if step == 0:
            fac_first[...] = fac[...]
        elif step == 1:
            for start, strip in strips:
                pair_hi[strip, :], pair_lo[strip, :] = halves(
                    narrow_dot(fac[strip, :], fac_first[...])
                )

    def rows_out(slot):
        return pltpu.make_async_remote_copy(
            src_ref=upd.at[slot * rows : (slot + 1) * rows, :],
            dst_ref=ret_ref.at[me],
            send_sem=out_send.at[slot],
            recv_sem=out_recv.at[me],
            device_id=(holder(slot), lane),
            device_id_type=MESH,
        )

    def write(slot):
        place = pl.ds(pl.multiple_of(holder(slot) * rows, rows), rows)
        return pltpu.make_async_copy(
            upd.at[slot * rows : (slot + 1) * rows, :], upd_ref.at[place, :], write_sem.at[slot]
        )

    own = pltpu.make_async_copy(upd.at[0:rows, :], ret_ref.at[me], own_sem.at[0])
    for start, strip in strips:
        high, low = halves(
            (narrow_dot(fac[strip, :], pair_hi[...]) + narrow_dot(fac[strip, :], pair_lo[...]))
            * (scale_out * inv_norm)
        )
        whole_hi[strip, :] = high
        whole_lo[strip, :] = low
        for top in range(start, start + half, 2 * rows):

            def apply_chunk(index, carry, top=top):
                place = pl.ds(pl.multiple_of(index * chunk, chunk), chunk)
                block = columns(index, 0, n)
                upd[top : top + 2 * rows, place] = (
                    narrow_dot(whole_hi[top : top + 2 * rows, :], block)
                    + narrow_dot(whole_lo[top : top + 2 * rows, :], block)
                ).astype(jnp.bfloat16)
                return carry

            lax.fori_loop(0, chunks, apply_chunk, 0)
            for slot in (top // rows, top // rows + 1):
                if slot:
                    start_in_turn(slot, lambda slot: rows_out(slot).start())
                else:
                    own.start()
    for slot in range(n):
        write(slot).start()

    for slot in range(1, n):
        rows_in(slot).wait_send()
    own.wait()
    for slot in range(n):
        write(slot).wait()
    for slot in range(1, n):
        rows_out(slot).wait_send()
        source = lax.rem(me + slot, n)
        pltpu.make_async_remote_copy(
            src_ref=upd.at[0:rows, :],
            dst_ref=ret_ref.at[source],
            send_sem=out_send.at[slot],
            recv_sem=out_recv.at[source],
            device_id=(source, lane),
            device_id_type=MESH,
        ).wait_recv()


def owner_call(scale_out, n, momentum, owner_order):
    rows, cols = momentum.shape[1:]
    size, first, strip = n * rows, (n - 2) * rows, 2 * rows

    def wide(*shape):
        return pltpu.VMEM(shape, jnp.float32)

    def narrow(*shape):
        return pltpu.VMEM(shape, jnp.bfloat16)

    def gram_buffers(height, width):
        return [
            wide(height, width), narrow(height, width), narrow(height, width),
            narrow(height // 2, width), narrow(height // 2, width), wide(height, width),
        ]

    dma = pltpu.SemaphoreType.DMA
    return pl.pallas_call(
        functools.partial(owner_kernel, n, rows, cols, cols // 4, scale_out),
        out_shape=(
            jax.ShapeDtypeStruct((n, rows, cols), jnp.bfloat16),
            jax.ShapeDtypeStruct((size, cols), jnp.bfloat16),
        ),
        in_specs=[
            pl.BlockSpec(memory_space=pltpu.SMEM),
            pl.BlockSpec(memory_space=pltpu.VMEM),
        ],
        out_specs=(pl.BlockSpec(memory_space=pl.ANY), pl.BlockSpec(memory_space=pl.ANY)),
        scratch_shapes=[
            narrow(n, rows, cols), narrow(n, rows, cols), narrow(size, cols), narrow(size, size),
            *gram_buffers(first, first),
            *gram_buffers(strip, size),
            *[narrow(size, size)] * 7,
            dma((n,)), dma((n,)), dma((6,)), dma((6,)), dma((n,)), dma((n,)), dma((1,)), dma((n,)),
        ],
        compiler_params=pltpu.CompilerParams(
            collective_id=0, has_side_effects=True, vmem_limit_bytes=32 << 20
        ),
        cost_estimate=pl.CostEstimate(
            flops=6 * size * size * cols + 40 * size**3,
            bytes_accessed=12 * size * cols,
            transcendentals=0,
        ),
    )(owner_order, momentum)


def master_kernel(n, order_ref, ret_ref, upd_ref, master_ref, out_ref, upd_out_ref, fresh, sems):
    whole = pltpu.make_async_copy(upd_ref, upd_out_ref, sems.at[n])
    copies = []
    for slot in range(n):
        matrix = order_ref[slot]
        fresh[slot] = master_ref[matrix] * (1.0 - learn_rate * weight_decay) - learn_rate * ret_ref[
            slot
        ].astype(jnp.float32)
        copies.append(pltpu.make_async_copy(fresh.at[slot], out_ref.at[matrix], sems.at[slot]))
        copies[-1].start()
        if slot == 0:
            whole.start()
    for copy in copies + [whole]:
        copy.wait()


def master_call(returned, update, master, owner_order):
    n = master.shape[0]
    vmem = pl.BlockSpec(memory_space=pltpu.VMEM)
    hbm = pl.BlockSpec(memory_space=pl.ANY)
    return pl.pallas_call(
        functools.partial(master_kernel, n),
        out_shape=(
            jax.ShapeDtypeStruct(master.shape, jnp.float32),
            jax.ShapeDtypeStruct(update.shape, update.dtype),
        ),
        in_specs=[pl.BlockSpec(memory_space=pltpu.SMEM), vmem, vmem, vmem],
        out_specs=(hbm, hbm),
        scratch_shapes=[
            pltpu.VMEM(master.shape, jnp.float32), pltpu.SemaphoreType.DMA((n + 1,))
        ],
        compiler_params=pltpu.CompilerParams(vmem_limit_bytes=24 << 20),
    )(owner_order, returned, update, master)


def kernel_shards(scale_out, n, momentum, master, owner_order):
    returned, owned_update = owner_call(scale_out, n, momentum, owner_order)
    new_master, owned_update = master_call(returned, owned_update, master, owner_order)
    return new_master, owned_update[None]


def wide_dot(left, right):
    return jnp.dot(left, right, precision=lax.Precision.HIGH)


def polynomial(gram):
    eye = jnp.eye(gram.shape[0], dtype=jnp.float32)
    whole = None
    for step in range(ITERS):
        factor = (
            quintic_first * eye + quintic_second * gram + quintic_third * wide_dot(gram, gram)
        )
        whole = factor if whole is None else wide_dot(factor, whole)
        if step + 1 < ITERS:
            gram = wide_dot(wide_dot(factor, gram), factor)
    return whole


def plain_shards(scale_out, momentum, master, owner_order):
    matrices = momentum.shape[0]
    slotted = jnp.take(momentum, owner_order, axis=0)
    owned = lax.all_to_all(slotted, "dp", split_axis=0, concat_axis=1, tiled=True)

    def one(matrix):
        squares = lax.psum(jnp.sum(jnp.square(matrix.astype(jnp.float32))), "tensor")
        inv_norm = 1.0 / (jnp.sqrt(squares) + norm_epsilon)
        partial_value = lax.dot_general(
            matrix, matrix, (((1,), (1,)), ((), ())), preferred_element_type=jnp.float32
        )
        gram = lax.psum(partial_value.astype(jnp.bfloat16), "tensor").astype(jnp.float32)
        whole = polynomial(gram * (inv_norm * inv_norm)) * (scale_out * inv_norm)
        return wide_dot(whole, matrix.astype(jnp.float32)).astype(jnp.bfloat16)

    owned_update = jnp.stack([one(owned[index]) for index in range(owned.shape[0])])
    returned = lax.all_to_all(owned_update, "dp", split_axis=1, concat_axis=0, tiled=True)
    inverse = (
        jnp.zeros((matrices,), jnp.int32).at[owner_order].set(jnp.arange(matrices, dtype=jnp.int32))
    )
    by_matrix = jnp.take(returned, inverse, axis=0)
    new_master = master * (1.0 - learn_rate * weight_decay) - learn_rate * by_matrix.astype(
        jnp.float32
    )
    return (new_master, owned_update)


def solution(mesh):
    n, lanes = mesh.shape["dp"], mesh.shape["tensor"]

    def whole_call(momentum, master, owner_order):
        scale_out = 0.2 * math.sqrt(max(momentum.shape[1], momentum.shape[2]))

        def shards(momentum, master, owner_order):
            matrices, rows, cols = momentum.shape
            if matrices == n and lanes == 4 and n >= 8 and n % 4 == 0 and rows % 64 == 0 and cols % 512 == 0:
                return kernel_shards(scale_out, n, momentum, master, owner_order)
            return plain_shards(scale_out, momentum, master, owner_order)

        return jax.shard_map(
            shards,
            mesh=mesh,
            in_specs=(P(None, "dp", "tensor"), P(None, "dp", "tensor"), P()),
            out_specs=(P(None, "dp", "tensor"), P("dp", None, "tensor")),
            check_vma=False,
        )(momentum, master, owner_order)

    return whole_call
```
